256 devices in a mesh: row: 8 (over z), col: 32 (over y, x, core).
Axes of the slice: x: 4, y: 4, z: 8, core: 2. Of those that a mesh axis runs over, the one named last changes fastest.
Arguments:
- flow_state: float32 [125, 5, 32768], P(None, None, ('row', 'col'))
- cot_final: float32 [125, 5, 32768], P(None, None, ('row', 'col')), may hold values from -6 to 6
- metric: float32 [32768], P(('row', 'col')), may hold values from 1 to 4
- send_col: int32 [256, 160], P(('row', 'col')), may hold values from 0 to 768, as said below
- send_row: int32 [256, 64], P(('row', 'col')), may hold values from 0 to 768, as said below
- exterior: int32 [256, 768], P(('row', 'col')), may hold values from 0 to 991, as said below
- face_kind: int32 [256, 768], P(('row', 'col')), may hold values from 0 to 3, as said below
- mortar_fine: int32 [256, 128], P(('row', 'col')), may hold values from 0 to 768, as said below
- mortar_coarse: int32 [256, 32], P(('row', 'col')), may hold values from 0 to 768, as said below
Outputs:
- cot_state: float32 [125, 5, 32768], P(None, None, ('row', 'col'))
The draws below stay inside these ranges and needn't reach their ends.
Inputs may be any that keep to these rules, and one draw needn't show every extreme that they name: `send_col`: each device lists, for each col peer h in order, 5 slots: slots 0 to 1 hold its +x faces whose partner is a -x face of h, the next 2 its -x faces whose partner is a +x face of h, the last 1 its +z faces that are coarse sides of mortars whose fine faces lie on h (slot 4 + i is mortar i of the pair); partners are listed in the same order on both sides; unused slots hold 768; some pair of devices fills every slot. `send_row`: likewise for row peers: slots 0 to 3 hold +y faces paired with -y faces of the peer, the next 4 -y faces paired with +y faces; unused slots hold 768. `exterior`: for a conforming face, the position of its partner's trace in the device's table; partners are symmetric and have opposite normals; wall and mortar faces name themselves. `face_kind`: 0 conforming, 1 wall, 2 fine side of a mortar (a -z face), 3 coarse side of a mortar (a +z face). `mortar_fine`: entry q * 32 + h + i is the fine face of quadrant q of mortar i whose coarse face lies on col peer h; mortars of a pair are numbered from 0; unused entries hold 768; every fine face appears at most once. `mortar_coarse`: entry h + i is the coarse face of mortar i whose fine faces lie on col peer h; unused entries hold 768.
All inputs are finite; a program needn't handle non-finite values.
Results may differ from the reference program's by a relative error of at most 0.0003.
Values sent between devices are 32-bit elements; how exact they have to be, the bound alone decides.
A program may use at most 128 MiB of HBM per device.

```python
import math
import jax
import jax.numpy as jnp
import numpy as np
from jax import lax

DEG = 4
FIELDS = 5
ELEM_DEV = 128
NODES = 125
LINKS = 2
LINKS_ROW = 4
MORTARS = 1
SLOTS = 5
SLOTS_ROW = 8
ELEMS = 32768
N_ROW = 8
N_COL = 32


GAMMA = 1.4


def draw_flow_state(key, part):
    subkeys = jax.random.split(key, 4)
    shape_one = (NODES, ELEMS)
    density = jnp.exp(jax.random.uniform(subkeys[0], shape_one, jnp.float32, -0.2, 0.2))
    velocity = 0.3 * jnp.clip(jax.random.normal(subkeys[1], (3, NODES, ELEMS), jnp.float32), -3.0, 3.0)
    pressure = jnp.exp(jax.random.uniform(subkeys[2], shape_one, jnp.float32, -0.3, 0.3))
    momentum = density[None] * velocity
    energy = pressure / (GAMMA - 1.0) + 0.5 * density * jnp.sum(velocity * velocity, axis=0)
    return jnp.stack([density, momentum[0], momentum[1], momentum[2], energy], axis=1).astype(jnp.float32)


def matched(key, groups, members):
    subkeys = jax.random.split(key, groups)
    shuffled = jax.vmap(lambda subkey: jax.random.permutation(subkey, members))(subkeys)
    position = jnp.argsort(shuffled, axis=1, stable=True)
    return jnp.take_along_axis(shuffled, position ^ 1, axis=1)


def link_counts(key, groups, members, bound_links):
    first_key, second_key = jax.random.split(key)
    random_counts = jax.random.randint(first_key, (groups, members, members), 0, bound_links + 1)
    partners = matched(second_key, groups, members)
    counter = jnp.arange(members)
    random_counts = jnp.where(counter[None, None, :] == partners[:, :, None], bound_links, random_counts)
    random_counts = jnp.where((counter[:, None] == counter[None, :])[None], 0, random_counts)
    return random_counts.astype(jnp.int32)


def offsets(counts):
    cumulative = jnp.cumsum(counts)
    return (cumulative, cumulative - counts, cumulative[-1])


def conform_side(order_plus, order_minus, out_counts, in_counts, base_minus, slot_base, stride, link_slots, elements):
    position = jnp.arange(elements, dtype=jnp.int32)
    base_plus = base_minus + elements
    pad_value = 6 * elements
    peer_count = out_counts.shape[0]
    out_cum, out_off, out_total = offsets(out_counts)
    in_cum, in_off, in_total = offsets(in_counts)
    paired = jnp.minimum(elements - out_total, elements - in_total)
    peer_plus = jnp.minimum(jnp.sum(position[:, None] >= out_cum[None, :], axis=1), peer_count - 1)
    rest_plus = position - out_total
    mate_plus = base_minus + order_minus[jnp.clip(in_total + rest_plus, 0, elements - 1)]
    remote_plus = slot_base + peer_plus * stride + link_slots + position - out_off[peer_plus]
    value_plus = jnp.where(position < out_total, remote_plus, jnp.where(rest_plus < paired, mate_plus, base_plus + order_plus))
    kind_plus = jnp.where((position < out_total) | (rest_plus < paired), 0, 1)
    peer_minus = jnp.minimum(jnp.sum(position[:, None] >= in_cum[None, :], axis=1), peer_count - 1)
    rest_minus = position - in_total
    mate_minus = base_plus + order_plus[jnp.clip(out_total + rest_minus, 0, elements - 1)]
    remote_minus = slot_base + peer_minus * stride + position - in_off[peer_minus]
    value_minus = jnp.where(position < in_total, remote_minus, jnp.where(rest_minus < paired, mate_minus, base_minus + order_minus))
    kind_minus = jnp.where((position < in_total) | (rest_minus < paired), 0, 1)
    ext_plus = jnp.zeros(elements, jnp.int32).at[order_plus].set(value_plus)
    ext_minus = jnp.zeros(elements, jnp.int32).at[order_minus].set(value_minus)
    kinds_plus = jnp.zeros(elements, jnp.int32).at[order_plus].set(kind_plus)
    kinds_minus = jnp.zeros(elements, jnp.int32).at[order_minus].set(kind_minus)
    slot_index = jnp.arange(link_slots, dtype=jnp.int32)
    plus_send = jnp.where(slot_index[None, :] < out_counts[:, None], base_plus + order_plus[jnp.clip(out_off[:, None] + slot_index[None, :], 0, elements - 1)], pad_value)
    minus_send = jnp.where(slot_index[None, :] < in_counts[:, None], base_minus + order_minus[jnp.clip(in_off[:, None] + slot_index[None, :], 0, elements - 1)], pad_value)
    return (ext_minus, ext_plus, kinds_minus, kinds_plus, jnp.concatenate([plus_send, minus_send], axis=1))


def mortar_side(order_plus, order_minus, out_counts, in_counts, mortar_slots, elements):
    position = jnp.arange(elements, dtype=jnp.int32)
    base_minus = 4 * elements
    base_plus = 5 * elements
    pad_value = 6 * elements
    out_cum, out_off, out_total = offsets(out_counts)
    in_cum, in_off, in_total = offsets(4 * in_counts)
    paired = jnp.minimum(elements - out_total, elements - in_total)
    rest_plus = position - out_total
    rest_minus = position - in_total
    local_plus = (rest_plus >= 0) & (rest_plus < paired)
    local_minus = (rest_minus >= 0) & (rest_minus < paired)
    value_plus = jnp.where(local_plus, base_minus + order_minus[jnp.clip(in_total + rest_plus, 0, elements - 1)], base_plus + order_plus)
    value_minus = jnp.where(local_minus, base_plus + order_plus[jnp.clip(out_total + rest_minus, 0, elements - 1)], base_minus + order_minus)
    kind_plus = jnp.where(position < out_total, 3, jnp.where(local_plus, 0, 1))
    kind_minus = jnp.where(position < in_total, 2, jnp.where(local_minus, 0, 1))
    ext_plus = jnp.zeros(elements, jnp.int32).at[order_plus].set(value_plus)
    ext_minus = jnp.zeros(elements, jnp.int32).at[order_minus].set(value_minus)
    kinds_plus = jnp.zeros(elements, jnp.int32).at[order_plus].set(kind_plus)
    kinds_minus = jnp.zeros(elements, jnp.int32).at[order_minus].set(kind_minus)
    slot_index = jnp.arange(mortar_slots, dtype=jnp.int32)
    quarter = jnp.arange(4, dtype=jnp.int32)
    coarse_list = jnp.where(slot_index[None, :] < out_counts[:, None], base_plus + order_plus[jnp.clip(out_off[:, None] + slot_index[None, :], 0, elements - 1)], pad_value)
    fine_index = in_off[None, :, None] + 4 * slot_index[None, None, :] + quarter[:, None, None]
    fine_list = jnp.where(slot_index[None, None, :] < in_counts[None, :, None], base_minus + order_minus[jnp.clip(fine_index, 0, elements - 1)], pad_value)
    return (ext_minus, ext_plus, kinds_minus, kinds_plus, coarse_list, fine_list)


def build_mesh(key):
    elements = ELEM_DEV
    rows = N_ROW
    cols = N_COL
    devices = rows * cols
    subkeys = jax.random.split(key, 4)
    col_links = link_counts(subkeys[0], rows, cols, LINKS)
    row_links = link_counts(subkeys[1], cols, rows, LINKS_ROW)
    hanging = link_counts(subkeys[2], rows, cols, MORTARS)
    order_keys = jax.random.split(subkeys[3], devices * 6)
    orders = jax.vmap(lambda subkey: jax.random.permutation(subkey, elements))(order_keys).astype(jnp.int32).reshape(devices, 6, elements)
    x_out = col_links.reshape(devices, cols)
    x_in = col_links.transpose(0, 2, 1).reshape(devices, cols)
    y_out = row_links.transpose(1, 0, 2).reshape(devices, rows)
    y_in = row_links.transpose(2, 0, 1).reshape(devices, rows)
    z_out = hanging.reshape(devices, cols)
    z_in = hanging.transpose(0, 2, 1).reshape(devices, cols)

    def per_device(order_set, xo_counts, xi_counts, yo_counts, yi_counts, zo_counts, zi_counts):
        col_base = 6 * elements
        row_base = col_base + cols * SLOTS
        x_minus, x_plus, kx_minus, kx_plus, x_send = conform_side(order_set[1], order_set[0], xo_counts, xi_counts, 0, col_base, SLOTS, LINKS, elements)
        y_minus, y_plus, ky_minus, ky_plus, y_send = conform_side(order_set[3], order_set[2], yo_counts, yi_counts, 2 * elements, row_base, SLOTS_ROW, LINKS_ROW, elements)
        z_minus, z_plus, kz_minus, kz_plus, coarse_list, fine_list = mortar_side(order_set[5], order_set[4], zo_counts, zi_counts, MORTARS, elements)
        outside = jnp.concatenate([x_minus, x_plus, y_minus, y_plus, z_minus, z_plus])
        kinds_all = jnp.concatenate([kx_minus, kx_plus, ky_minus, ky_plus, kz_minus, kz_plus])
        col_send = jnp.concatenate([x_send, coarse_list], axis=1).reshape(-1)
        return (col_send, y_send.reshape(-1), outside, kinds_all, fine_list.reshape(-1), coarse_list.reshape(-1))
    made = jax.vmap(per_device)(orders, x_out, x_in, y_out, y_in, z_out, z_in)
    return tuple((item.astype(jnp.int32) for item in made))


def draw_send_col(key, part):
    return build_mesh(jax.random.fold_in(key, 11))[0]


def draw_send_row(key, part):
    return build_mesh(jax.random.fold_in(key, 11))[1]


def draw_exterior(key, part):
    return build_mesh(jax.random.fold_in(key, 11))[2]


def draw_face_kind(key, part):
    return build_mesh(jax.random.fold_in(key, 11))[3]


def draw_mortar_fine(key, part):
    return build_mesh(jax.random.fold_in(key, 11))[4]


def draw_mortar_coarse(key, part):
    return build_mesh(jax.random.fold_in(key, 11))[5]


def levels(own_key, extent, cuts, low, top_value):
    def one(axis_at, parts):
        draws = jax.random.uniform(jax.random.fold_in(jax.random.fold_in(own_key, 6), axis_at), (parts,), jnp.float32, low / len(cuts), top_value / len(cuts))
        return jnp.repeat(jnp.exp(draws), extent[axis_at] // parts).reshape((-1,) + (1,) * (len(extent) - axis_at - 1))

    level = one(*cuts[0])
    for cut in cuts[1:]:
        level = level * one(*cut)
    return level


def bell_draw(rng, extent, spread, reach, cuts=(), kind=jnp.bfloat16):
    values = spread * jax.random.normal(rng, extent, jnp.float32)
    if cuts:
        values = values * levels(rng, extent, cuts, -0.22, 0.18)
    return jnp.clip(values, -reach, reach).astype(kind)


def setup_inputs(seed: int = 0) -> dict:
    splits = jax.random.split(jax.random.key(seed), 10)
    flow_state = draw_flow_state(jax.random.fold_in(splits[9], 71), 0)
    cot_final = bell_draw(splits[1], (NODES, FIELDS, ELEMS), 1.0, 6.0, ((2, 256),), jnp.float32)
    metric = jnp.clip(jnp.exp(math.log(4.0) - 1.3862944 * jax.random.uniform(splits[2], (ELEMS,), jnp.float32) ** levels(splits[2], (ELEMS,), ((0, 256),), -0.2, 0.2)), 1.0, 4.0)
    send_col = draw_send_col(jax.random.fold_in(splits[9], 71), 0)
    send_row = draw_send_row(jax.random.fold_in(splits[9], 71), 0)
    exterior = draw_exterior(jax.random.fold_in(splits[9], 71), 0)
    face_kind = draw_face_kind(jax.random.fold_in(splits[9], 71), 0)
    mortar_fine = draw_mortar_fine(jax.random.fold_in(splits[9], 71), 0)
    mortar_coarse = draw_mortar_coarse(jax.random.fold_in(splits[9], 71), 0)
    return {"flow_state": flow_state, "cot_final": cot_final, "metric": metric, "send_col": send_col, "send_row": send_row, "exterior": exterior, "face_kind": face_kind, "mortar_fine": mortar_fine, "mortar_coarse": mortar_coarse}


GAMMA = 1.4
STEP = 0.005
HIGH = lax.Precision.HIGHEST

def lobatto_rule(degree):
    if degree == 2:
        return ([-1.0, 0.0, 1.0], [1.0 / 3.0, 4.0 / 3.0, 1.0 / 3.0])
    if degree == 3:
        inner = math.sqrt(0.2)
        return ([-1.0, -inner, inner, 1.0], [1.0 / 6.0, 5.0 / 6.0, 5.0 / 6.0, 1.0 / 6.0])
    inner = math.sqrt(3.0 / 7.0)
    return ([-1.0, -inner, 0.0, inner, 1.0], [0.1, 49.0 / 90.0, 32.0 / 45.0, 49.0 / 90.0, 0.1])

def basis_tables(degree):
    size_one = degree + 1
    point_list, weight_list = lobatto_rule(degree)
    points = np.array(point_list)
    weights = np.array(weight_list)

    def lagrange(where_at):
        result = np.ones((len(where_at), size_one))
        for column in range(size_one):
            for other_node in range(size_one):
                if other_node != column:
                    result[:, column] *= (where_at - points[other_node]) / (points[column] - points[other_node])
        return result
    identity_one = np.eye(size_one)
    node_gaps = points[:, None] - points[None, :] + identity_one
    barycentric = 1.0 / np.prod(node_gaps, axis=1)
    derivative = barycentric[None, :] / barycentric[:, None] / node_gaps * (1.0 - identity_one)
    derivative = derivative - identity_one * derivative.sum(axis=1)[:, None]
    halves = [lagrange((points + 2.0 * half_index - 1.0) / 2.0) for half_index in (0, 1)]
    projections = [0.5 * (matrix.T * weights[None, :]) / weights[:, None] for matrix in halves]
    identity_two = np.eye(size_one * size_one)
    along = np.concatenate([np.kron(identity_two, derivative), np.kron(np.kron(identity_one, derivative), identity_one), np.kron(derivative, identity_two)], axis=1)
    interp = np.stack([np.kron(halves[first_half], halves[second_half]) for first_half in (0, 1) for second_half in (0, 1)])
    project = np.stack([np.kron(projections[first_half], projections[second_half]) for first_half in (0, 1) for second_half in (0, 1)])
    return (jnp.asarray(along, jnp.float32), jnp.asarray(interp, jnp.float32), jnp.asarray(project, jnp.float32), float(weights[0]))

def euler_flux(flow_field, direction, orient):
    density = flow_field[:, 0]
    momentum = flow_field[:, 1:4]
    energy = flow_field[:, 4]
    velocity = momentum / density[:, None]
    pressure = (GAMMA - 1.0) * (energy - 0.5 * lax.optimization_barrier(jnp.sum(momentum * velocity, axis=1)))
    normal = velocity[:, direction]
    pieces = [momentum[:, direction]]
    for component in range(3):
        flux_term = momentum[:, component] * normal
        if component == direction:
            flux_term = flux_term + pressure
        pieces.append(flux_term)
    pieces.append((energy + pressure) * normal)
    return (orient * jnp.stack(pieces, axis=1), normal, GAMMA * pressure / density)

def rusanov(left_state, right_state, direction, orient):
    flux_left, normal_left, sound_left = euler_flux(left_state, direction, orient)
    flux_right, normal_right, sound_right = euler_flux(right_state, direction, orient)
    speed = jnp.sqrt(0.5 * (normal_left * normal_left + normal_right * normal_right) + 0.5 * (sound_left + sound_right))
    return (0.5 * (flux_left + flux_right) - 0.5 * speed[:, None] * (right_state - left_state), flux_left)

def reflect(flow_field, direction):
    factor = jnp.where(jnp.arange(5) == direction + 1, -1.0, 1.0).astype(flow_field.dtype)
    return flow_field * factor[None, :, None]

def face_traces(flow_field):
    side_nodes = DEG + 1
    fields_count = flow_field.shape[1]
    elements = flow_field.shape[2]
    volume_grid = flow_field.reshape(side_nodes, side_nodes, side_nodes, fields_count, elements)
    blocks = [volume_grid[:, :, 0], volume_grid[:, :, side_nodes - 1], volume_grid[:, 0], volume_grid[:, side_nodes - 1], volume_grid[0], volume_grid[side_nodes - 1]]
    stacked = jnp.stack([block.reshape(side_nodes * side_nodes, fields_count, elements) for block in blocks], axis=2)
    return stacked.reshape(side_nodes * side_nodes, fields_count, 6 * elements)

def spread_faces(face_values):
    side_nodes = DEG + 1
    face_size, fields_count, total_faces = face_values.shape
    elements = total_faces // 6
    blocks = face_values.reshape(face_size, fields_count, 6, elements)

    def block_at(face_index):
        return blocks[:, :, face_index].reshape(side_nodes, side_nodes, fields_count, elements)
    volume_grid = jnp.zeros((side_nodes, side_nodes, side_nodes, fields_count, elements), face_values.dtype)
    volume_grid = volume_grid.at[:, :, 0].add(block_at(0))
    volume_grid = volume_grid.at[:, :, side_nodes - 1].add(block_at(1))
    volume_grid = volume_grid.at[:, 0].add(block_at(2))
    volume_grid = volume_grid.at[:, side_nodes - 1].add(block_at(3))
    volume_grid = volume_grid.at[0].add(block_at(4))
    volume_grid = volume_grid.at[side_nodes - 1].add(block_at(5))
    return volume_grid.reshape(side_nodes ** 3, fields_count, elements)

def face_fluxes(traces, outside, face_kinds):
    elements = traces.shape[2] // 6
    stars = []
    owns = []
    for face_index in range(6):
        direction = face_index // 2
        orient = 2.0 * (face_index % 2) - 1.0
        window = slice(face_index * elements, (face_index + 1) * elements)
        own_trace = traces[:, :, window]
        joined, own_flux = rusanov(own_trace, outside[:, :, window], direction, orient)
        walled = rusanov(own_trace, reflect(own_trace, direction), direction, orient)[0]
        stars.append(jnp.where(face_kinds[window][None, None, :] == 1, walled, joined))
        owns.append(own_flux)
    return (jnp.concatenate(stars, axis=2), jnp.concatenate(owns, axis=2))

def coarse_slots(received, peer_count):
    face_size, fields_count, width = received.shape
    shaped = received.reshape(face_size, fields_count, peer_count, SLOTS)[:, :, :, 2 * LINKS:]
    return shaped.reshape(face_size, fields_count, peer_count * MORTARS)

def mortar_fluxes(traces, coarse, fine_list, tables):
    along, interp, project, weight_end = tables
    fine_traces = jnp.take(traces, fine_list, axis=2, mode='clip')
    spread_quarters = jnp.concatenate([jnp.einsum('ab,bfm->afm', interp[quarter], coarse, precision=HIGH) for quarter in range(4)], axis=2)
    mortar_flux = rusanov(fine_traces, spread_quarters, 2, -1.0)[0]
    face_size, fields_count, total = mortar_flux.shape
    quarters = mortar_flux.reshape(face_size, fields_count, 4, total // 4)
    sent_back = jnp.zeros((face_size, fields_count, total // 4), mortar_flux.dtype)
    for quarter in range(4):
        sent_back = sent_back - jnp.einsum('ab,bfm->afm', project[quarter], quarters[:, :, quarter], precision=HIGH)
    return (mortar_flux, sent_back)

def volume_rate(flow_field, metric, tables):
    along = tables[0]
    node_count, fields_count, elements = flow_field.shape
    stacked = jnp.concatenate([euler_flux(flow_field, direction, 1.0)[0] for direction in range(3)], axis=0)
    summed = jnp.dot(along, stacked.reshape(3 * node_count, fields_count * elements), precision=HIGH, preferred_element_type=jnp.float32)
    return -metric[None, None, :] * summed.reshape(node_count, fields_count, elements)

def assemble(flow_field, metric, traces, outside, face_kinds, fine_flux, fine_list, returned, coarse_list, tables):
    weight_end = tables[3]
    stars, owns = face_fluxes(traces, outside, face_kinds)
    stars = stars.at[:, :, fine_list].set(fine_flux, mode='drop')
    stars = stars.at[:, :, coarse_list].set(returned, mode='drop')
    face_scale = jnp.tile(metric, 6) / weight_end
    correction = (owns - stars) * face_scale[None, None, :]
    return volume_rate(flow_field, metric, tables) + spread_faces(correction)

def swap_cols(blocks):
    devices, face_size, fields_count, width = blocks.shape
    block_width = width // N_COL
    shaped = blocks.reshape(N_ROW, N_COL, face_size, fields_count, N_COL, block_width)
    return jnp.swapaxes(shaped, 1, 4).reshape(devices, face_size, fields_count, width)

def swap_rows(blocks):
    devices, face_size, fields_count, width = blocks.shape
    block_width = width // N_ROW
    shaped = blocks.reshape(N_ROW, N_COL, face_size, fields_count, N_ROW, block_width)
    return jnp.swapaxes(shaped, 0, 4).reshape(devices, face_size, fields_count, width)

def reference(flow_state, cot_final, metric, send_col, send_row, exterior, face_kind, mortar_fine, mortar_coarse):
    tables = basis_tables(DEG)
    devices = N_ROW * N_COL
    metrics = metric.reshape(devices, ELEM_DEV)

    def split_devices(whole_field):
        return whole_field.reshape(NODES, FIELDS, devices, ELEM_DEV).transpose(2, 0, 1, 3)

    def join_devices(per_device):
        return per_device.transpose(1, 2, 0, 3).reshape(NODES, FIELDS, devices * ELEM_DEV)

    def outgoing(packed):
        flow_field, col_list, row_list = packed
        traces = face_traces(flow_field)
        return (jnp.take(traces, col_list, axis=2, mode='clip'), jnp.take(traces, row_list, axis=2, mode='clip'))

    def mortar_back(packed):
        flow_field, got_col, fine_list = packed
        return mortar_fluxes(face_traces(flow_field), coarse_slots(got_col, N_COL), fine_list, tables)[1]

    def device_rate(packed):
        flow_field, metric_dev, got_col, got_row, returned, outside_list, kinds_dev, fine_list, coarse_list = packed
        traces = face_traces(flow_field)
        trace_table = jnp.concatenate([traces, got_col, got_row], axis=2)
        outside = jnp.take(trace_table, outside_list, axis=2)
        fine_flux = mortar_fluxes(traces, coarse_slots(got_col, N_COL), fine_list, tables)[0]
        return assemble(flow_field, metric_dev, traces, outside, kinds_dev, fine_flux, fine_list, returned, coarse_list, tables)

    def section(whole_field):
        per_device = split_devices(whole_field)
        sent_col, sent_row = lax.map(jax.checkpoint(outgoing), (per_device, send_col, send_row))
        got_col = swap_cols(sent_col)
        got_row = swap_rows(sent_row)
        mortar_backs = lax.map(jax.checkpoint(mortar_back), (per_device, got_col, mortar_fine))
        returned = swap_cols(mortar_backs)
        device_rates = lax.map(jax.checkpoint(device_rate), (per_device, metrics, got_col, got_row, returned, exterior, face_kind, mortar_fine, mortar_coarse))
        return join_devices(device_rates)

    def advance(initial):
        middle = initial + STEP * section(initial)
        return 0.5 * initial + 0.5 * (middle + STEP * section(middle))
    unused, pullback = jax.vjp(advance, flow_state)
    return pullback(cot_final)[0]
```

```python
import functools
import math

import jax
import jax.numpy as jnp
import numpy as np
from jax import lax
from jax.experimental import pallas as pl
from jax.experimental.pallas import tpu as pltpu
from jax.sharding import PartitionSpec as P

STEP = 0.005
W_END = 0.1
COL_ROWS = 16
ROW_ROWS = 8
LANES = 128
GROUPS = 7
WIDE = GROUPS * LANES
MESH = pl.DeviceIdType.MESH
F32 = jnp.float32
BF16 = jnp.bfloat16
FIELD_ORDER = ((0, 1, 2, 3, 4), (0, 2, 1, 3, 4), (0, 3, 1, 2, 4))


def basis():
    inner = math.sqrt(3.0 / 7.0)
    x = np.array([-1.0, -inner, 0.0, inner, 1.0])
    w = np.array([0.1, 49.0 / 90.0, 32.0 / 45.0, 49.0 / 90.0, 0.1])

    def lagrange(at):
        out = np.ones((5, 5))
        for m in range(5):
            for n in range(5):
                if n != m:
                    out[:, m] *= (at - x[n]) / (x[m] - x[n])
        return out

    eye = np.eye(5)
    gaps = x[:, None] - x[None, :] + eye
    bary = 1.0 / np.prod(gaps, axis=1)
    diff = bary[None, :] / bary[:, None] / gaps * (1.0 - eye)
    diff = diff - eye * diff.sum(axis=1)[:, None]
    halves = [lagrange((x + 2.0 * a - 1.0) / 2.0) for a in (0, 1)]
    projs = [0.5 * (m.T * w[None, :]) / w[:, None] for m in halves]
    interp = [np.kron(halves[a], halves[b]) for a in (0, 1) for b in (0, 1)]
    project = [np.kron(projs[a], projs[b]) for a in (0, 1) for b in (0, 1)]
    return diff, interp, project


def stencil_tables():
    diff = basis()[0]
    parts = []
    for matrix in (diff, diff.T):
        along = np.zeros((5, 8))
        along[:, :5] = matrix.T
        parts.append(along.reshape(40))
        parts.append(np.repeat(matrix.reshape(25), 8))
    column = np.concatenate(parts)
    return np.repeat(column[:, None], LANES, axis=1).astype(np.float32)


def mortar_tables():
    _, interp, project = basis()
    out = np.zeros((4, 4, LANES, LANES))
    for q in range(4):
        for at, matrix in enumerate(
            (interp[q], project[q].T, project[q], interp[q].T)
        ):
            out[at, q, :125, :125] = np.kron(np.eye(5), matrix)
    out = out.reshape(4, 4 * LANES, LANES).astype(np.float32)
    high = out.astype(jnp.bfloat16)
    low = (out - high.astype(np.float32)).astype(jnp.bfloat16)
    return high, low


def split(x):
    high = x.astype(BF16)
    return high, (x - high.astype(F32)).astype(BF16)


def split_rows(x):
    return jnp.concatenate(split(x), axis=0)


def dot(a, b):
    return lax.dot_general(a, b, (((1,), (0,)), ((), ())), preferred_element_type=F32)


def dot_nt(a, b):
    return lax.dot_general(a, b, (((1,), (1,)), ((), ())), preferred_element_type=F32)


def pick(x, onehot):
    both = dot(split_rows(x), onehot)
    return both[: x.shape[0]] + both[x.shape[0] :]


def place(x, onehot):
    both = dot_nt(split_rows(x), onehot)
    return both[: x.shape[0]] + both[x.shape[0] :]


def rows_at(start, size=8):
    return pl.ds(pl.multiple_of(start, 8), size)


def kernel(
    nr, nc, send_width,
    u_ref, c_ref, met_ref, int_ref, tab_ref, khi_ref, klo_ref,
    out_ref,
    u1_ref, acc_ref, fz_ref, own_ref, ext_ref, val_ref, tc_ref, xc_ref, vc_ref,
    ohs_ref, ohr_ref, ohl_ref, lane_ref,
    sbuf, rbuf, send_sem, recv_sem,
):
    mr = lax.axis_index("row")
    mc = lax.axis_index("col")
    barrier = pltpu.get_barrier_semaphore()

    def greet_col(k, carry):
        pl.semaphore_signal(
            barrier, inc=1, device_id=(mr, lax.rem(mc + k, nc)), device_id_type=MESH
        )
        return carry

    def greet_row(k, carry):
        pl.semaphore_signal(
            barrier, inc=1, device_id=(lax.rem(mr + k, nr), mc), device_id_type=MESH
        )
        return carry

    lax.fori_loop(1, nc, greet_col, 0)
    lax.fori_loop(1, nr, greet_row, 0)

    chunks = send_width // LANES
    at_ext = chunks
    at_sel = at_ext + 6
    at_kind = at_sel + 2
    at_fine = at_kind + 6
    at_coarse = at_fine + 1
    moved_rows = COL_ROWS * (nc - 1) + ROW_ROWS * (nr - 1)

    def onehot(target, rows, base=0):
        iota = lax.broadcasted_iota(jnp.int32, (rows, LANES), 0) + base
        return jnp.where(iota == target, 1.0, 0.0).astype(BF16)

    for n in range(chunks):
        ohs_ref[:, n * LANES : (n + 1) * LANES] = onehot(int_ref[n : n + 1, :], 768)
    for k in range(6):
        target = int_ref[at_ext + k : at_ext + k + 1, :]
        ohl_ref[k] = onehot(target, LANES)
        remote = target if k < 4 else int_ref[at_sel + k - 4 : at_sel + k - 3, :] + LANES
        ohr_ref[:, k * LANES : (k + 1) * LANES] = onehot(remote, send_width, LANES)
    fine_list = int_ref[at_fine : at_fine + 1, :]
    coarse_list = int_ref[at_coarse : at_coarse + 1, :]
    ohl_ref[6] = onehot(fine_list - 512, LANES)
    ohl_ref[7] = onehot(coarse_list - 640, LANES)

    for k in range(GROUPS):
        lanes = slice(k * LANES, (k + 1) * LANES)
        one = jnp.ones((1, LANES), F32)
        if k < 6:
            kind = int_ref[at_kind + k : at_kind + k + 1, :]
            rows = [
                one * (2.0 * (k % 2) - 1.0),
                jnp.where(kind == 3, -1.0, 1.0),
                one,
                jnp.where((kind == 0) | (kind == 2), 1.0, 0.0),
                jnp.where(kind == 1, 1.0, 0.0),
                one,
                met_ref[...] * (1.0 / W_END),
            ]
        else:
            valid = jnp.where(coarse_list < 768, 1.0, 0.0)
            rows = [one, -one, -one, one, 0.0 * one, valid, one]
        for n, row in enumerate(rows):
            lane_ref[n : n + 1, lanes] = row

    for e in range(4):
        tc_ref[e, 120:128, :] = jnp.zeros((8, 768), F32)
        rbuf[e, nc * COL_ROWS + nr * ROW_ROWS :, :] = jnp.zeros(
            (send_width - nc * COL_ROWS - nr * ROW_ROWS, LANES), F32
        )
    vc_ref[120:128, :] = jnp.zeros((8, LANES), F32)


    def post(e, src_ref, scale):
        def take(a, carry):
            for k in range(6):
                d, h = k // 2, k % 2
                lanes = slice(k * LANES, (k + 1) * LANES)
                for f in range(5):
                    base = 200 * FIELD_ORDER[d][f]
                    if d == 0:
                        piece = src_ref[pl.ds(base + 40 * a + 4 * h, 5, 8), :]
                    elif d == 1:
                        piece = src_ref[rows_at(base + 40 * a + 32 * h), :]
                    else:
                        piece = src_ref[rows_at(base + 160 * h + 8 * a), :]
                    if scale is not None:
                        piece = piece * (met_ref[...] * (scale / W_END))
                    own_ref[e, 5 * f + a, : piece.shape[0], lanes] = piece
            return carry

        lax.fori_loop(0, 5, take, 0)
        for g in range(25):
            tc_ref[e, 5 * g : 5 * g + 5, :] = own_ref[e, g, 0:5, 0:768]
        both = split_rows(tc_ref[e])
        sent = dot(both, ohs_ref[...])
        sent = sent[:LANES] + sent[LANES:]
        for n in range(chunks):
            sbuf[e, n * LANES : (n + 1) * LANES, :] = sent[:, n * LANES : (n + 1) * LANES].T
        if e == 0:
            pl.semaphore_wait(barrier, nc + nr - 2)

        def push_col(k, carry):
            peer = lax.rem(mc + k, nc)
            pltpu.make_async_remote_copy(
                src_ref=sbuf.at[e, rows_at(COL_ROWS * peer, COL_ROWS)],
                dst_ref=rbuf.at[e, rows_at(COL_ROWS * mc, COL_ROWS)],
                send_sem=send_sem.at[e],
                recv_sem=recv_sem.at[e],
                device_id=(mr, peer),
                device_id_type=MESH,
            ).start()
            return carry

        def push_row(k, carry):
            peer = lax.rem(mr + k, nr)
            pltpu.make_async_remote_copy(
                src_ref=sbuf.at[e, rows_at(COL_ROWS * nc + ROW_ROWS * peer, ROW_ROWS)],
                dst_ref=rbuf.at[e, rows_at(COL_ROWS * nc + ROW_ROWS * mr, ROW_ROWS)],
                send_sem=send_sem.at[e],
                recv_sem=recv_sem.at[e],
                device_id=(peer, mc),
                device_id_type=MESH,
            ).start()
            return carry

        lax.fori_loop(1, nc, push_col, 0)
        lax.fori_loop(1, nr, push_row, 0)
        own_col = rows_at(COL_ROWS * mc, COL_ROWS)
        rbuf[e, own_col, :] = sbuf[e, own_col, :]
        own_row = rows_at(COL_ROWS * nc + ROW_ROWS * mr, ROW_ROWS)
        rbuf[e, own_row, :] = sbuf[e, own_row, :]
        for k in range(6):
            other = k ^ 1
            got = dot(both[:, other * LANES : (other + 1) * LANES], ohl_ref[k])
            xc_ref[e, :, k * LANES : (k + 1) * LANES] = got[:LANES] + got[LANES:]
        got = dot(both[:, 5 * LANES : 6 * LANES], ohl_ref[7])
        xc_ref[e, :, 7 * LANES :] = got[:LANES] + got[LANES:]

    quarter = lax.broadcasted_iota(jnp.int32, (1, LANES), 1) // nc

    def by_quarter(at, x):
        width = x.shape[1] // LANES
        hi, lo = split(x)
        k_hi, k_lo = khi_ref[at], klo_ref[at]
        full = dot(k_hi, hi) + (dot(k_lo, hi) + dot(k_hi, lo))
        out = []
        for n in range(width):
            total = jnp.zeros((LANES, LANES), F32)
            for q in range(4):
                block = full[q * LANES : (q + 1) * LANES, n * LANES : (n + 1) * LANES]
                total = total + jnp.where(quarter == q, block, 0.0)
            out.append(total)
        return out

    def finish(e, table):
        size = pl.ds(0, moved_rows)
        whole = pltpu.make_async_copy(sbuf.at[e, size], rbuf.at[e, size], recv_sem.at[e])
        whole.wait()
        came = jnp.concatenate(
            [rbuf[e, n * LANES : (n + 1) * LANES, :].T for n in range(chunks)], axis=1
        )
        got = pick(came, ohr_ref[...])
        for k in range(4):
            lanes = slice(k * LANES, (k + 1) * LANES)
            xc_ref[e, :, lanes] = xc_ref[e, :, lanes] + got[:, lanes]
        xc_ref[e, :, 6 * LANES : 7 * LANES] = got[:, 5 * LANES :]
        coarse = jnp.concatenate([got[:, 4 * LANES : 5 * LANES], xc_ref[e, :, 7 * LANES :]], axis=1)
        fine_side, coarse_side = by_quarter(table, coarse)
        lanes = slice(4 * LANES, 5 * LANES)
        xc_ref[e, :, lanes] = xc_ref[e, :, lanes] + place(fine_side, ohl_ref[6])
        xc_ref[e, :, 7 * LANES :] = coarse_side
        for g in range(25):
            ext_ref[e, g] = xc_ref[e, 5 * g : 5 * g + 8, 0:WIDE]
            own_ref[e, g, :, 6 * LANES :] = xc_ref[e, 5 * g : 5 * g + 8, WIDE:]

    def sent_all(e):
        size = pl.ds(0, moved_rows)
        pltpu.make_async_copy(sbuf.at[e, size], rbuf.at[e, size], send_sem.at[e]).wait()


    def lane_row(n):
        return lane_ref[n : n + 1, :]

    def both_states(e, a):
        own = [own_ref[e, 5 * f + a] for f in range(5)]
        ext = [ext_ref[e, 5 * f + a] for f in range(5)]
        return own, ext

    def fill_states(e, a):
        own, ext = both_states(e, a)
        gathered = lane_row(3) > 0.5
        valid = lane_row(5) > 0.5
        flip = 1.0 - 2.0 * lane_row(4)
        default = (1.0, 0.0, 0.0, 0.0, 1.0)
        own = [jnp.where(valid, own[f], default[f]) for f in range(5)]
        mirror = [own[f] * flip if f == 1 else own[f] for f in range(5)]
        ext = [jnp.where(gathered, ext[f], mirror[f]) for f in range(5)]
        ext = [jnp.where(valid, ext[f], default[f]) for f in range(5)]
        return own, ext

    def primitives(s):
        inv = 1.0 / s[0]
        vel = [s[1] * inv, s[2] * inv, s[3] * inv]
        square = vel[0] * vel[0] + vel[1] * vel[1] + vel[2] * vel[2]
        pressure = 0.4 * (s[4] - 0.5 * (s[1] * vel[0] + s[2] * vel[1] + s[3] * vel[2]))
        return inv, vel, square, pressure

    def face_flux(e):
        def body(a, carry):
            own, ext = fill_states(e, a)
            orient, sign = lane_row(0), lane_row(1)
            fluxes, parts = [], []
            for s in (own, ext):
                inv, vel, _, pressure = primitives(s)
                fluxes.append(
                    (
                        s[1],
                        s[1] * vel[0] + pressure,
                        s[2] * vel[0],
                        s[3] * vel[0],
                        (s[4] + pressure) * vel[0],
                    )
                )
                parts.append(vel[0] * vel[0] + 1.4 * pressure * inv)
            speed = jnp.sqrt(0.5 * (parts[0] + parts[1]))
            for f in range(5):
                val_ref[5 * f + a] = 0.5 * (
                    orient * (fluxes[0][f] - sign * fluxes[1][f])
                    + sign * speed * (ext[f] - own[f])
                )
            return carry

        lax.fori_loop(0, 5, body, 0)

    def face_adjoint(state, cot):
        def body(a, carry):
            own, ext = fill_states(state, a)
            y, y_ext = both_states(cot, a)
            gathered = lane_row(3) > 0.5
            flip = 1.0 - 2.0 * lane_row(4)
            y_ext = [
                jnp.where(gathered, y_ext[f], y[f] * flip if f == 1 else y[f]) for f in range(5)
            ]
            orient, sign = lane_row(0), lane_row(2)
            inv, vel, square, pressure = primitives(own)
            inv_b, vel_b, _, pressure_b = primitives(ext)
            sound = 1.4 * pressure * inv
            speed2 = 0.5 * (
                vel[0] * vel[0] + vel_b[0] * vel_b[0] + sound + 1.4 * pressure_b * inv_b
            )
            speed = jnp.sqrt(speed2)
            plus = [orient * (y_ext[f] + sign * y[f]) for f in range(5)]
            minus = [y[f] - y_ext[f] for f in range(5)]
            dots = minus[0] * (ext[0] - own[0])
            for f in range(1, 5):
                dots = dots + minus[f] * (ext[f] - own[f])
            spread = 0.5 * dots * inv / speed
            p_bar = plus[1] + plus[4] * vel[0]
            along = plus[1] * vel[0] + plus[2] * vel[1] + plus[3] * vel[2]
            along = along + plus[4] * (own[4] + pressure) * inv
            v_n = vel[0]
            result = [
                -v_n * along
                + 0.2 * square * p_bar
                + spread * (0.14 * square - v_n * v_n - 0.5 * sound),
                v_n * plus[1] - 0.4 * v_n * p_bar + plus[0] + along + 0.72 * spread * v_n,
                v_n * plus[2] - vel[1] * (0.4 * p_bar + 0.28 * spread),
                v_n * plus[3] - vel[2] * (0.4 * p_bar + 0.28 * spread),
                plus[4] * v_n + 0.4 * p_bar + 0.28 * spread,
            ]
            for f in range(5):
                val_ref[5 * f + a] = 0.5 * (result[f] - speed * minus[f])
            return carry

        lax.fori_loop(0, 5, body, 0)

    def coarse_sum(table, factor):
        for g in range(25):
            vc_ref[5 * g : 5 * g + 5, :] = val_ref[g, 0:5, 6 * LANES :]
        (summed,) = by_quarter(table, vc_ref[...])
        back = place(summed, ohl_ref[7])
        vc_ref[...] = back
        for g in range(25):
            val_ref[g, :, 5 * LANES : 6 * LANES] = (
                val_ref[g, :, 5 * LANES : 6 * LANES] + factor * vc_ref[5 * g : 5 * g + 8, :]
            )
        vc_ref[120:128, :] = jnp.zeros((8, LANES), F32)

    def spread_faces(scale):
        def body(a, carry):
            for k in range(6):
                d, h = k // 2, k % 2
                lanes = slice(k * LANES, (k + 1) * LANES)
                for f in range(5):
                    base = 200 * FIELD_ORDER[d][f]
                    size = 5 if d == 0 else 8
                    piece = val_ref[5 * f + a, 0:size, lanes]
                    if scale is not None:
                        piece = piece * scale
                    if d == 0:
                        where = pl.ds(base + 40 * a + 4 * h, 5, 8)
                    elif d == 1:
                        where = rows_at(base + 40 * a + 32 * h)
                    else:
                        where = rows_at(base + 160 * h + 8 * a)
                    acc_ref[where, :] = acc_ref[where, :] + piece
            return carry

        lax.fori_loop(0, 5, body, 0)


    diff = basis()[0]

    def slab_along(x, transposed):
        base = 240 if transposed else 0
        total = None
        for m in range(5):
            term = tab_ref[base + 8 * m : base + 8 * m + 8, :] * x[:, m : m + 1, :]
            total = term if total is None else total + term
        return total

    def slab_across(x, transposed):
        matrix = diff.T if transposed else diff
        rows = []
        for k in range(5):
            total = float(matrix[k, 0]) * x[0]
            for m in range(1, 5):
                if matrix[k, m] != 0.0:
                    total = total + float(matrix[k, m]) * x[m]
            rows.append(total[None])
        return jnp.concatenate(rows, axis=0)

    def slab_stack(ref, f, level, transposed):
        base = 280 if transposed else 40
        total = None
        for m in range(5):
            coef = tab_ref[rows_at(base + 40 * level + 8 * m), :]
            term = coef[None] * slab(ref, f, m)
            total = term if total is None else total + term
        return total

    def slab(ref, f, level):
        return ref[rows_at(200 * f + 40 * level, 40), :].reshape(5, 8, LANES)

    def put(ref, f, level, x):
        ref[rows_at(200 * f + 40 * level, 40), :] = x.reshape(40, LANES)

    def volume_forward():
        def first(level, carry):
            s = [slab(u_ref, f, level) for f in range(5)]
            _, vel, _, pressure = primitives(s)
            total = s[4] + pressure

            def flux(d, f):
                if f == 0:
                    return s[d + 1]
                if f == 4:
                    return total * vel[d]
                term = s[f] * vel[d]
                return term + pressure if f == d + 1 else term

            for f in range(5):
                put(fz_ref, f, level, flux(2, f))
                put(
                    acc_ref, f, level,
                    slab_along(flux(0, f), False) + slab_across(flux(1, f), False),
                )
            return carry

        def second(level, carry):
            for f in range(5):
                total = slab(acc_ref, f, level) + slab_stack(fz_ref, f, level, False)
                put(acc_ref, f, level, total * (-met_ref[...])[None])
            return carry

        lax.fori_loop(0, 5, first, 0)
        lax.fori_loop(0, 5, second, 0)

    def volume_adjoint(state_ref, cot_ref, scale):
        def body(level, carry):
            s = [slab(state_ref, f, level) for f in range(5)]
            inv, vel, square, pressure = primitives(s)
            enthalpy = (s[4] + pressure) * inv
            factor = (met_ref[...] * (-scale))[None]
            out = [None] * 5
            p_sum = None
            extra = []

            def add(f, x):
                out[f] = x if out[f] is None else out[f] + x

            for d in range(3):
                w = []
                for f in range(5):
                    if d == 0:
                        w.append(slab_along(slab(cot_ref, f, level), True))
                    elif d == 1:
                        w.append(slab_across(slab(cot_ref, f, level), True))
                    else:
                        w.append(slab_stack(cot_ref, f, level, True))
                p_bar = w[d + 1] + w[4] * vel[d]
                p_sum = p_bar if p_sum is None else p_sum + p_bar
                along = w[1] * vel[0] + w[2] * vel[1] + w[3] * vel[2] + w[4] * enthalpy
                for k in range(3):
                    add(k + 1, vel[d] * w[k + 1])
                extra.append(w[0] + along)
                add(0, -vel[d] * along)
                add(4, w[4] * vel[d])
            add(0, 0.2 * square * p_sum)
            add(4, 0.4 * p_sum)
            for k in range(3):
                add(k + 1, extra[k] - 0.4 * vel[k] * p_sum)
            for f in range(5):
                put(acc_ref, f, level, out[f] * factor)
            return carry

        lax.fori_loop(0, 5, body, 0)


    post(0, u_ref, None)
    post(1, c_ref, 0.5 * STEP)
    volume_forward()
    finish(0, 0)
    face_flux(0)
    coarse_sum(2, -1.0)
    spread_faces(met_ref[...] * (1.0 / W_END))
    for f in range(5):
        at = slice(200 * f, 200 * f + 200)
        u1_ref[at, :] = u_ref[at, :] + STEP * acc_ref[at, :]
    post(2, u1_ref, None)
    volume_adjoint(u1_ref, c_ref, 0.5 * STEP)
    finish(1, 1)
    finish(2, 0)
    face_adjoint(2, 1)
    coarse_sum(3, 1.0)
    spread_faces(None)
    for f in range(5):
        at = slice(200 * f, 200 * f + 200)
        u1_ref[at, :] = 0.5 * c_ref[at, :] + acc_ref[at, :]
    post(3, u1_ref, STEP)
    volume_adjoint(u_ref, u1_ref, STEP)
    finish(3, 1)
    face_adjoint(0, 3)
    coarse_sum(3, 1.0)
    spread_faces(None)
    for f in range(5):
        at = slice(200 * f, 200 * f + 200)
        out_ref[at, :] = (0.5 * c_ref[at, :] + u1_ref[at, :]) + acc_ref[at, :]
    for e in range(4):
        sent_all(e)


def on_device(
    nr, nc, flow_state, cot_final, metric,
    send_col, send_row, exterior, face_kind, mortar_fine, mortar_coarse,
):
    used = nc * COL_ROWS + nr * ROW_ROWS
    send_width = -(-used // LANES) * LANES

    def by_field(x):
        x = x.reshape(25, 5, 5, LANES).transpose(2, 0, 1, 3)
        x = jnp.pad(x, ((0, 0), (0, 0), (0, 3), (0, 0)), constant_values=1.0)
        return x.reshape(1000, LANES)

    none = 768
    slots = jnp.concatenate(
        [
            send_col[0].reshape(nc, 5),
            mortar_fine[0].reshape(4, nc).T,
            jnp.full((nc, COL_ROWS - 9), none, jnp.int32),
        ],
        axis=1,
    ).reshape(-1)
    slots = jnp.concatenate(
        [slots, send_row[0], jnp.full(send_width - used, none, jnp.int32)]
    ).reshape(-1, LANES)
    ext = exterior[0].reshape(6, LANES)
    kind = face_kind[0].reshape(6, LANES)
    col_base, row_base = 768, 768 + 5 * nc
    partner = jnp.array([[k ^ 1] for k in range(6)], jnp.int32) * LANES
    in_col = ext - col_base
    peer = in_col // 5
    row_of = jnp.where(
        ext < col_base,
        ext - partner,
        jnp.where(
            ext < row_base,
            LANES + COL_ROWS * peer + (in_col - 5 * peer),
            LANES + COL_ROWS * nc + (ext - row_base),
        ),
    )
    row_of = jnp.where(kind == 0, row_of, -1)
    lane = np.arange(LANES)
    inside = lane < 4 * nc
    choose = np.stack(
        [
            np.where(inside, COL_ROWS * (lane % nc) + 4, -1000),
            np.where(inside, COL_ROWS * (lane % nc) + 5 + lane // nc, -1000),
        ]
    ).astype(np.int32)
    short = jnp.full(LANES - 4 * nc, none, jnp.int32)
    fine = jnp.concatenate([mortar_fine[0], short])[None]
    coarse = jnp.concatenate([jnp.tile(mortar_coarse[0], 4), short])[None]
    ints = jnp.concatenate([slots, row_of, choose, kind, fine, coarse], axis=0)
    k_high, k_low = mortar_tables()

    vmem = pl.BlockSpec(memory_space=pltpu.VMEM)
    out = pl.pallas_call(
        functools.partial(kernel, nr, nc, send_width),
        out_shape=jax.ShapeDtypeStruct((1000, LANES), F32),
        in_specs=[vmem] * 7,
        out_specs=vmem,
        scratch_shapes=[
            pltpu.VMEM((1000, LANES), F32),
            pltpu.VMEM((1000, LANES), F32),
            pltpu.VMEM((1000, LANES), F32),
            pltpu.VMEM((4, 25, 8, WIDE), F32),
            pltpu.VMEM((4, 25, 8, WIDE), F32),
            pltpu.VMEM((25, 8, WIDE), F32),
            pltpu.VMEM((4, LANES, 768), F32),
            pltpu.VMEM((4, LANES, 8 * LANES), F32),
            pltpu.VMEM((LANES, LANES), F32),
            pltpu.VMEM((768, send_width), BF16),
            pltpu.VMEM((send_width, 768), BF16),
            pltpu.VMEM((8, LANES, LANES), BF16),
            pltpu.VMEM((8, WIDE), F32),
            pltpu.VMEM((4, send_width, LANES), F32),
            pltpu.VMEM((4, send_width, LANES), F32),
            pltpu.SemaphoreType.DMA((4,)),
            pltpu.SemaphoreType.DMA((4,)),
        ],
        compiler_params=pltpu.CompilerParams(
            collective_id=0, has_side_effects=True, vmem_limit_bytes=40 * 2**20
        ),
    )(
        by_field(flow_state),
        by_field(cot_final),
        metric.reshape(1, LANES),
        ints,
        jnp.asarray(stencil_tables()),
        jnp.asarray(k_high),
        jnp.asarray(k_low),
    )
    out = out.reshape(5, 25, 8, LANES)[:, :, :5]
    return out.transpose(1, 2, 0, 3).reshape(125, 5, LANES)


def solution(mesh):
    both = ("row", "col")
    in_specs = (P(None, None, both), P(None, None, both), P(both)) + (P(both, None),) * 6
    return jax.shard_map(
        functools.partial(on_device, mesh.shape["row"], mesh.shape["col"]),
        mesh=mesh,
        in_specs=in_specs,
        out_specs=P(None, None, both),
        check_vma=False,
    )
```

```python
import functools
import math

import jax
import jax.numpy as jnp
import numpy as np
from jax import lax
from jax.experimental import pallas as pl
from jax.experimental.pallas import tpu as pltpu
from jax.sharding import PartitionSpec as P

STEP = 0.005
W_END = 0.1
COL_ROWS = 16
ROW_ROWS = 8
LANES = 128
GROUPS = 7
WIDE = GROUPS * LANES
MESH = pl.DeviceIdType.MESH
F32 = jnp.float32
BF16 = jnp.bfloat16
FIELD_ORDER = ((0, 1, 2, 3, 4), (0, 2, 1, 3, 4), (0, 3, 1, 2, 4))


def basis():
    inner = math.sqrt(3.0 / 7.0)
    x = np.array([-1.0, -inner, 0.0, inner, 1.0])
    w = np.array([0.1, 49.0 / 90.0, 32.0 / 45.0, 49.0 / 90.0, 0.1])

    def lagrange(at):
        out = np.ones((5, 5))
        for m in range(5):
            for n in range(5):
                if n != m:
                    out[:, m] *= (at - x[n]) / (x[m] - x[n])
        return out

    eye = np.eye(5)
    gaps = x[:, None] - x[None, :] + eye
    bary = 1.0 / np.prod(gaps, axis=1)
    diff = bary[None, :] / bary[:, None] / gaps * (1.0 - eye)
    diff = diff - eye * diff.sum(axis=1)[:, None]
    halves = [lagrange((x + 2.0 * a - 1.0) / 2.0) for a in (0, 1)]
    projs = [0.5 * (m.T * w[None, :]) / w[:, None] for m in halves]
    interp = [np.kron(halves[a], halves[b]) for a in (0, 1) for b in (0, 1)]
    project = [np.kron(projs[a], projs[b]) for a in (0, 1) for b in (0, 1)]
    return diff, interp, project


def stencil_tables():
    diff = basis()[0]
    parts = []
    for matrix in (diff, diff.T):
        along = np.zeros((5, 8))
        along[:, :5] = matrix.T
        parts.append(along.reshape(40))
        parts.append(np.repeat(matrix.reshape(25), 8))
    column = np.concatenate(parts)
    return np.repeat(column[:, None], LANES, axis=1).astype(np.float32)


def mortar_tables():
    _, interp, project = basis()
    out = np.zeros((4, 4, LANES, LANES))
    for q in range(4):
        for at, matrix in enumerate(
            (interp[q], project[q].T, project[q], interp[q].T)
        ):
            out[at, q, :125, :125] = np.kron(np.eye(5), matrix)
    out = out.reshape(4, 4 * LANES, LANES).astype(np.float32)
    high = out.astype(jnp.bfloat16)
    low = (out - high.astype(np.float32)).astype(jnp.bfloat16)
    return high, low


def split(x):
    high = x.astype(BF16)
    return high, (x - high.astype(F32)).astype(BF16)


def split_rows(x):
    return jnp.concatenate(split(x), axis=0)


def dot(a, b):
    return lax.dot_general(a, b, (((1,), (0,)), ((), ())), preferred_element_type=F32)


def dot_nt(a, b):
    return lax.dot_general(a, b, (((1,), (1,)), ((), ())), preferred_element_type=F32)


def pick(x, onehot):
    both = dot(split_rows(x), onehot)
    return both[: x.shape[0]] + both[x.shape[0] :]


def place(x, onehot):
    both = dot_nt(split_rows(x), onehot)
    return both[: x.shape[0]] + both[x.shape[0] :]


def rows_at(start, size=8):
    return pl.ds(pl.multiple_of(start, 8), size)


def kernel(
    nr, nc,
    u_hbm, c_hbm, met_hbm, col_hbm, row_hbm, ext_hbm, kind_hbm, fine_hbm, coarse_hbm,
    tab_hbm, khi_hbm, klo_hbm,
    out_ref,
    un_ref, cn_ref, met_ref, col_ref, row_ref, exterior_ref, kind_ref, fine_ref, coarse_ref,
    tab_ref, khi_ref, klo_ref,
    u_ref, c_ref, u1_ref, acc_ref, fz_ref, own_ref, ext_ref, val_ref, tc_ref, xc_ref, vc_ref,
    list_ref, ohs_ref, ohr_ref, ohl_ref, lane_ref, slot_ref, came_ref,
    sbuf, rbuf, load_sem, send_sem, recv_sem,
):
    mr = lax.axis_index("row")
    mc = lax.axis_index("col")
    loads = [
        pltpu.make_async_copy(src, dst, load_sem.at[n])
        for n, (src, dst) in enumerate(
            (
                (u_hbm, un_ref),
                (met_hbm, met_ref),
                (col_hbm, col_ref),
                (row_hbm, row_ref),
                (fine_hbm, fine_ref),
                (coarse_hbm, coarse_ref),
                (ext_hbm, exterior_ref),
                (kind_hbm, kind_ref),
                (c_hbm, cn_ref),
                (tab_hbm, tab_ref),
                (khi_hbm, khi_ref),
                (klo_hbm, klo_ref),
            )
        )
    ]
    for load in loads:
        load.start()
    barrier = pltpu.get_barrier_semaphore()

    def greet_col(k, carry):
        pl.semaphore_signal(
            barrier, inc=1, device_id=(mr, lax.rem(mc + k, nc)), device_id_type=MESH
        )
        return carry

    def greet_row(k, carry):
        pl.semaphore_signal(
            barrier, inc=1, device_id=(lax.rem(mr + k, nr), mc), device_id_type=MESH
        )
        return carry

    lax.fori_loop(1, nc, greet_col, 0)
    lax.fori_loop(1, nr, greet_row, 0)

    moved_rows = 9 * (nc - 1) + ROW_ROWS * (nr - 1)
    row_base = COL_ROWS * nc


    for e in range(4):
        tc_ref[e, 120:128, :] = jnp.zeros((8, 768), F32)
    vc_ref[120:128, :] = jnp.zeros((8, LANES), F32)
    came_ref[...] = jnp.zeros((4 * LANES, LANES), F32)
    for load in loads[:8]:
        load.wait()

    def natural(ref, wide_ref):
        for g in range(24):
            for f in range(5):
                at = 200 * f + 8 * g
                wide_ref[at : at + 8, :] = ref[f, 5 * g : 5 * g + 8, :]
        for f in range(5):
            at = 200 * f + 192
            wide_ref[at : at + 8, :] = jnp.ones((8, LANES), F32)
            wide_ref[at : at + 5, :] = ref[f, 120:125, :]

    natural(un_ref, u_ref)

    def onehot(target, base=0):
        iota = lax.broadcasted_iota(jnp.int32, (LANES, LANES), 0) + base
        return jnp.where(iota == target, 1.0, 0.0).astype(BF16)

    list_ref[...] = jnp.full((1, 5 * LANES), 768, jnp.int32)
    list_ref[:, 0 : 5 * nc] = col_ref[...]
    list_ref[:, 2 * LANES : 2 * LANES + 4 * nc] = fine_ref[...]
    list_ref[:, 3 * LANES : 3 * LANES + 8 * nr] = row_ref[...]
    for q in range(4):
        list_ref[:, 4 * LANES + q * nc : 4 * LANES + (q + 1) * nc] = coarse_ref[...]

    def listed(n):
        return list_ref[:, n * LANES : (n + 1) * LANES]

    coarse_list = listed(4)
    for n, k in enumerate((0, 1, 5)):
        for half in range(2):
            ohs_ref[n * LANES : (n + 1) * LANES, half * LANES : (half + 1) * LANES] = onehot(
                listed(half), k * LANES
            )
    for n, k in enumerate((2, 3)):
        ohs_ref[(3 + n) * LANES : (4 + n) * LANES, 0:LANES] = onehot(listed(3), k * LANES)
    for k in range(6):
        lanes = slice(k * LANES, (k + 1) * LANES)
        at = exterior_ref[:, lanes]
        near = (kind_ref[:, lanes] == 0) & (at < 768)
        ohl_ref[k] = onehot(jnp.where(near, at - (k ^ 1) * LANES, -1))
        far = (kind_ref[:, lanes] == 0) & (at >= 768)
        half = slice((k % 2) * LANES, (k % 2 + 1) * LANES)
        if k < 2:
            at = at - 768
            peer = (at * 205) >> 10
            at = (at - 5 * peer) * nc + peer
            ohr_ref[0:LANES, half] = onehot(jnp.where(far, at, -1))
        elif k < 4:
            ohr_ref[LANES:, half] = onehot(jnp.where(far, at - 768 - 5 * nc, -1))
    ohl_ref[6] = onehot(listed(2), 4 * LANES)
    ohl_ref[7] = onehot(coarse_list, 5 * LANES)

    for k in range(GROUPS):
        lanes = slice(k * LANES, (k + 1) * LANES)
        one = jnp.ones((1, LANES), F32)
        if k < 6:
            kind = kind_ref[:, lanes]
            rows = [
                one * (2.0 * (k % 2) - 1.0),
                jnp.where(kind == 3, -1.0, 1.0),
                one,
                jnp.where((kind == 0) | (kind == 2), 1.0, 0.0),
                jnp.where(kind == 1, 1.0, 0.0),
                one,
            ]
        else:
            valid = jnp.where(coarse_list < 768, 1.0, 0.0)
            rows = [one, -one, -one, one, 0.0 * one, valid]
        for n, row in enumerate(rows):
            lane_ref[n : n + 1, lanes] = row


    def post(e, src_ref, scale):
        def take(a, carry):
            for k in range(6):
                d, h = k // 2, k % 2
                lanes = slice(k * LANES, (k + 1) * LANES)
                for f in range(5):
                    base = 200 * FIELD_ORDER[d][f]
                    if d == 0:
                        piece = src_ref[pl.ds(base + 40 * a + 4 * h, 5, 8), :]
                    elif d == 1:
                        piece = src_ref[rows_at(base + 40 * a + 32 * h), :]
                    else:
                        piece = src_ref[rows_at(base + 160 * h + 8 * a), :]
                    if scale is not None:
                        piece = piece * (met_ref[...] * (scale / W_END))
                    own_ref[e, 5 * f + a, : piece.shape[0], lanes] = piece
            return carry

        lax.fori_loop(0, 5, take, 0)
        for g in range(25):
            tc_ref[e, 5 * g : 5 * g + 5, :] = own_ref[e, g, 0:5, 0:768]
        both = split_rows(tc_ref[e])

        def group(k, count=1):
            return both[:, k * LANES : (k + count) * LANES]

        def listed_rows(at, x):
            x = x[:LANES] + x[LANES:]
            for n in range(x.shape[1] // LANES):
                slot_ref[at + n * LANES : at + (n + 1) * LANES, :] = x[:, n * LANES : (n + 1) * LANES].T

        listed_rows(0, dot(group(0, 2), ohs_ref[0:256, :]) + dot(group(5), ohs_ref[256:384, :]))
        listed_rows(2 * LANES, dot(group(4), ohl_ref[6]))
        listed_rows(3 * LANES, dot(group(2, 2), ohs_ref[384:640, 0:LANES]))
        for n in range(5):
            sbuf[e, pl.ds(n, nc, COL_ROWS), :] = slot_ref[pl.ds(n, nc, 5), :]
        for q in range(4):
            sbuf[e, pl.ds(5 + q, nc, COL_ROWS), :] = slot_ref[2 * LANES + q * nc : 2 * LANES + (q + 1) * nc, :]
        sbuf[e, row_base : row_base + ROW_ROWS * nr, :] = slot_ref[3 * LANES : 3 * LANES + ROW_ROWS * nr, :]
        if e == 0:
            pl.semaphore_wait(barrier, nc + nr - 2)

        def push_col(k, carry):
            peer = lax.rem(mc + k, nc)
            pltpu.make_async_remote_copy(
                src_ref=sbuf.at[e, rows_at(COL_ROWS * peer, 9)],
                dst_ref=rbuf.at[e, rows_at(COL_ROWS * mc, 9)],
                send_sem=send_sem.at[e],
                recv_sem=recv_sem.at[e],
                device_id=(mr, peer),
                device_id_type=MESH,
            ).start()
            return carry

        def push_row(k, carry):
            peer = lax.rem(mr + k, nr)
            pltpu.make_async_remote_copy(
                src_ref=sbuf.at[e, rows_at(row_base + ROW_ROWS * peer, ROW_ROWS)],
                dst_ref=rbuf.at[e, rows_at(row_base + ROW_ROWS * mr, ROW_ROWS)],
                send_sem=send_sem.at[e],
                recv_sem=recv_sem.at[e],
                device_id=(peer, mc),
                device_id_type=MESH,
            ).start()
            return carry

        lax.fori_loop(1, nc, push_col, 0)
        lax.fori_loop(1, nr, push_row, 0)
        own_col = rows_at(COL_ROWS * mc, COL_ROWS)
        rbuf[e, own_col, :] = sbuf[e, own_col, :]
        own_row = rows_at(row_base + ROW_ROWS * mr, ROW_ROWS)
        rbuf[e, own_row, :] = sbuf[e, own_row, :]
        for k in range(6):
            got = dot(group(k ^ 1), ohl_ref[k])
            xc_ref[e, :, k * LANES : (k + 1) * LANES] = got[:LANES] + got[LANES:]
        got = dot(group(5), ohl_ref[7])
        xc_ref[e, :, 7 * LANES :] = got[:LANES] + got[LANES:]

    quarter = lax.broadcasted_iota(jnp.int32, (1, LANES), 1) // nc

    def by_quarter(at, x):
        width = x.shape[1] // LANES
        hi, lo = split(x)
        k_hi, k_lo = khi_ref[at], klo_ref[at]
        full = dot(k_hi, hi) + (dot(k_lo, hi) + dot(k_hi, lo))
        out = []
        for n in range(width):
            total = jnp.zeros((LANES, LANES), F32)
            for q in range(4):
                block = full[q * LANES : (q + 1) * LANES, n * LANES : (n + 1) * LANES]
                total = total + jnp.where(quarter == q, block, 0.0)
            out.append(total)
        return out

    def finish(e, table):
        size = pl.ds(0, moved_rows)
        whole = pltpu.make_async_copy(sbuf.at[e, size], rbuf.at[e, size], recv_sem.at[e])
        whole.wait()
        for n in range(4):
            came_ref[n * nc : (n + 1) * nc, :] = rbuf[e, pl.ds(n, nc, COL_ROWS), :]
        coarse = rbuf[e, pl.ds(4, nc, COL_ROWS), :]
        for q in range(4):
            came_ref[LANES + q * nc : LANES + (q + 1) * nc, :] = coarse
            came_ref[2 * LANES + q * nc : 2 * LANES + (q + 1) * nc, :] = rbuf[
                e, pl.ds(5 + q, nc, COL_ROWS), :
            ]
        came_ref[3 * LANES : 3 * LANES + ROW_ROWS * nr, :] = rbuf[e, row_base : row_base + ROW_ROWS * nr, :]
        for n, chunk in enumerate((0, 3)):
            got = pick(came_ref[chunk * LANES : (chunk + 1) * LANES, :].T, ohr_ref[n * LANES : (n + 1) * LANES, :])
            lanes = slice(2 * n * LANES, 2 * (n + 1) * LANES)
            xc_ref[e, :, lanes] = xc_ref[e, :, lanes] + got
        xc_ref[e, :, 6 * LANES : 7 * LANES] = came_ref[2 * LANES : 3 * LANES, :].T
        coarse = jnp.concatenate([came_ref[LANES : 2 * LANES, :].T, xc_ref[e, :, 7 * LANES :]], axis=1)
        fine_side, coarse_side = by_quarter(table, coarse)
        lanes = slice(4 * LANES, 5 * LANES)
        xc_ref[e, :, lanes] = xc_ref[e, :, lanes] + place(fine_side, ohl_ref[6])
        xc_ref[e, :, 7 * LANES :] = coarse_side
        for g in range(25):
            ext_ref[e, g] = xc_ref[e, 5 * g : 5 * g + 8, 0:WIDE]
            own_ref[e, g, :, 6 * LANES :] = xc_ref[e, 5 * g : 5 * g + 8, WIDE:]

    def sent_all(e):
        size = pl.ds(0, moved_rows)
        pltpu.make_async_copy(sbuf.at[e, size], rbuf.at[e, size], send_sem.at[e]).wait()


    def lane_row(n):
        return lane_ref[n : n + 1, :]

    def both_states(e, a):
        own = [own_ref[e, 5 * f + a] for f in range(5)]
        ext = [ext_ref[e, 5 * f + a] for f in range(5)]
        return own, ext

    def fill_states(e, a):
        own, ext = both_states(e, a)
        gathered = lane_row(3) > 0.5
        valid = lane_row(5) > 0.5
        flip = 1.0 - 2.0 * lane_row(4)
        default = (1.0, 0.0, 0.0, 0.0, 1.0)
        own = [jnp.where(valid, own[f], default[f]) for f in range(5)]
        mirror = [own[f] * flip if f == 1 else own[f] for f in range(5)]
        ext = [jnp.where(gathered, ext[f], mirror[f]) for f in range(5)]
        ext = [jnp.where(valid, ext[f], default[f]) for f in range(5)]
        return own, ext

    def primitives(s):
        inv = 1.0 / s[0]
        vel = [s[1] * inv, s[2] * inv, s[3] * inv]
        square = vel[0] * vel[0] + vel[1] * vel[1] + vel[2] * vel[2]
        pressure = 0.4 * (s[4] - 0.5 * (s[1] * vel[0] + s[2] * vel[1] + s[3] * vel[2]))
        return inv, vel, square, pressure

    def face_flux(e):
        def body(a, carry):
            own, ext = fill_states(e, a)
            orient, sign = lane_row(0), lane_row(1)
            fluxes, parts = [], []
            for s in (own, ext):
                inv, vel, _, pressure = primitives(s)
                fluxes.append(
                    (
                        s[1],
                        s[1] * vel[0] + pressure,
                        s[2] * vel[0],
                        s[3] * vel[0],
                        (s[4] + pressure) * vel[0],
                    )
                )
                parts.append(vel[0] * vel[0] + 1.4 * pressure * inv)
            speed = jnp.sqrt(0.5 * (parts[0] + parts[1]))
            for f in range(5):
                val_ref[5 * f + a] = 0.5 * (
                    orient * (fluxes[0][f] - sign * fluxes[1][f])
                    + sign * speed * (ext[f] - own[f])
                )
            return carry

        lax.fori_loop(0, 5, body, 0)

    def face_adjoint(state, cot):
        def body(a, carry):
            own, ext = fill_states(state, a)
            y, y_ext = both_states(cot, a)
            gathered = lane_row(3) > 0.5
            flip = 1.0 - 2.0 * lane_row(4)
            y_ext = [
                jnp.where(gathered, y_ext[f], y[f] * flip if f == 1 else y[f]) for f in range(5)
            ]
            orient, sign = lane_row(0), lane_row(2)
            inv, vel, square, pressure = primitives(own)
            inv_b, vel_b, _, pressure_b = primitives(ext)
            sound = 1.4 * pressure * inv
            speed2 = 0.5 * (
                vel[0] * vel[0] + vel_b[0] * vel_b[0] + sound + 1.4 * pressure_b * inv_b
            )
            speed = jnp.sqrt(speed2)
            plus = [orient * (y_ext[f] + sign * y[f]) for f in range(5)]
            minus = [y[f] - y_ext[f] for f in range(5)]
            dots = minus[0] * (ext[0] - own[0])
            for f in range(1, 5):
                dots = dots + minus[f] * (ext[f] - own[f])
            spread = 0.5 * dots * inv / speed
            p_bar = plus[1] + plus[4] * vel[0]
            along = plus[1] * vel[0] + plus[2] * vel[1] + plus[3] * vel[2]
            along = along + plus[4] * (own[4] + pressure) * inv
            v_n = vel[0]
            result = [
                -v_n * along
                + 0.2 * square * p_bar
                + spread * (0.14 * square - v_n * v_n - 0.5 * sound),
                v_n * plus[1] - 0.4 * v_n * p_bar + plus[0] + along + 0.72 * spread * v_n,
                v_n * plus[2] - vel[1] * (0.4 * p_bar + 0.28 * spread),
                v_n * plus[3] - vel[2] * (0.4 * p_bar + 0.28 * spread),
                plus[4] * v_n + 0.4 * p_bar + 0.28 * spread,
            ]
            for f in range(5):
                val_ref[5 * f + a] = 0.5 * (result[f] - speed * minus[f])
            return carry

        lax.fori_loop(0, 5, body, 0)

    def coarse_sum(table, factor):
        for g in range(25):
            vc_ref[5 * g : 5 * g + 5, :] = val_ref[g, 0:5, 6 * LANES :]
        (summed,) = by_quarter(table, vc_ref[...])
        back = place(summed, ohl_ref[7])
        vc_ref[...] = back
        for g in range(25):
            val_ref[g, :, 5 * LANES : 6 * LANES] = (
                val_ref[g, :, 5 * LANES : 6 * LANES] + factor * vc_ref[5 * g : 5 * g + 8, :]
            )
        vc_ref[120:128, :] = jnp.zeros((8, LANES), F32)

    def spread_faces(scale):
        def body(a, carry):
            for k in range(6):
                d, h = k // 2, k % 2
                lanes = slice(k * LANES, (k + 1) * LANES)
                for f in range(5):
                    base = 200 * FIELD_ORDER[d][f]
                    size = 5 if d == 0 else 8
                    piece = val_ref[5 * f + a, 0:size, lanes]
                    if scale is not None:
                        piece = piece * scale
                    if d == 0:
                        where = pl.ds(base + 40 * a + 4 * h, 5, 8)
                    elif d == 1:
                        where = rows_at(base + 40 * a + 32 * h)
                    else:
                        where = rows_at(base + 160 * h + 8 * a)
                    acc_ref[where, :] = acc_ref[where, :] + piece
            return carry

        lax.fori_loop(0, 5, body, 0)


    diff = basis()[0]

    def slab_along(x, transposed):
        base = 240 if transposed else 0
        total = None
        for m in range(5):
            term = tab_ref[base + 8 * m : base + 8 * m + 8, :] * x[:, m : m + 1, :]
            total = term if total is None else total + term
        return total

    def slab_across(x, transposed):
        matrix = diff.T if transposed else diff
        rows = []
        for k in range(5):
            total = float(matrix[k, 0]) * x[0]
            for m in range(1, 5):
                if matrix[k, m] != 0.0:
                    total = total + float(matrix[k, m]) * x[m]
            rows.append(total[None])
        return jnp.concatenate(rows, axis=0)

    def slab_stack(ref, f, level, transposed):
        base = 280 if transposed else 40
        total = None
        for m in range(5):
            coef = tab_ref[rows_at(base + 40 * level + 8 * m), :]
            term = coef[None] * slab(ref, f, m)
            total = term if total is None else total + term
        return total

    def slab(ref, f, level):
        return ref[rows_at(200 * f + 40 * level, 40), :].reshape(5, 8, LANES)

    def put(ref, f, level, x):
        ref[rows_at(200 * f + 40 * level, 40), :] = x.reshape(40, LANES)

    def volume_forward():
        def first(level, carry):
            s = [slab(u_ref, f, level) for f in range(5)]
            _, vel, _, pressure = primitives(s)
            total = s[4] + pressure

            def flux(d, f):
                if f == 0:
                    return s[d + 1]
                if f == 4:
                    return total * vel[d]
                term = s[f] * vel[d]
                return term + pressure if f == d + 1 else term

            for f in range(5):
                put(fz_ref, f, level, flux(2, f))
                put(
                    acc_ref, f, level,
                    slab_along(flux(0, f), False) + slab_across(flux(1, f), False),
                )
            return carry

        def second(level, carry):
            for f in range(5):
                total = slab(acc_ref, f, level) + slab_stack(fz_ref, f, level, False)
                put(acc_ref, f, level, total * (-met_ref[...])[None])
            return carry

        lax.fori_loop(0, 5, first, 0)
        lax.fori_loop(0, 5, second, 0)

    def volume_adjoint(state_ref, cot_ref, scale):
        def body(level, carry):
            s = [slab(state_ref, f, level) for f in range(5)]
            inv, vel, square, pressure = primitives(s)
            enthalpy = (s[4] + pressure) * inv
            factor = (met_ref[...] * (-scale))[None]
            out = [None] * 5
            p_sum = None
            extra = []

            def add(f, x):
                out[f] = x if out[f] is None else out[f] + x

            for d in range(3):
                w = []
                for f in range(5):
                    if d == 0:
                        w.append(slab_along(slab(cot_ref, f, level), True))
                    elif d == 1:
                        w.append(slab_across(slab(cot_ref, f, level), True))
                    else:
                        w.append(slab_stack(cot_ref, f, level, True))
                p_bar = w[d + 1] + w[4] * vel[d]
                p_sum = p_bar if p_sum is None else p_sum + p_bar
                along = w[1] * vel[0] + w[2] * vel[1] + w[3] * vel[2] + w[4] * enthalpy
                for k in range(3):
                    add(k + 1, vel[d] * w[k + 1])
                extra.append(w[0] + along)
                add(0, -vel[d] * along)
                add(4, w[4] * vel[d])
            add(0, 0.2 * square * p_sum)
            add(4, 0.4 * p_sum)
            for k in range(3):
                add(k + 1, extra[k] - 0.4 * vel[k] * p_sum)
            for f in range(5):
                put(acc_ref, f, level, out[f] * factor)
            return carry

        lax.fori_loop(0, 5, body, 0)


    post(0, u_ref, None)
    loads[8].wait()
    natural(cn_ref, c_ref)
    post(1, c_ref, 0.5 * STEP)
    loads[9].wait()
    volume_forward()
    loads[10].wait()
    loads[11].wait()
    finish(0, 0)
    face_flux(0)
    coarse_sum(2, -1.0)
    spread_faces(met_ref[...] * (1.0 / W_END))
    for f in range(5):
        at = slice(200 * f, 200 * f + 200)
        u1_ref[at, :] = u_ref[at, :] + STEP * acc_ref[at, :]
    post(2, u1_ref, None)
    volume_adjoint(u1_ref, c_ref, 0.5 * STEP)
    finish(1, 1)
    finish(2, 0)
    face_adjoint(2, 1)
    coarse_sum(3, 1.0)
    spread_faces(None)
    for f in range(5):
        at = slice(200 * f, 200 * f + 200)
        u1_ref[at, :] = 0.5 * c_ref[at, :] + acc_ref[at, :]
    post(3, u1_ref, STEP)
    volume_adjoint(u_ref, u1_ref, STEP)
    finish(3, 1)
    face_adjoint(0, 3)
    coarse_sum(3, 1.0)
    spread_faces(None)
    for g in range(25):
        for f in range(5):
            at = slice(200 * f + 8 * g, 200 * f + 8 * g + 5)
            out_ref[f, 5 * g : 5 * g + 5, :] = (0.5 * c_ref[at, :] + u1_ref[at, :]) + acc_ref[at, :]
    for e in range(4):
        sent_all(e)


def on_device(
    nr, nc, flow_state, cot_final, metric,
    send_col, send_row, exterior, face_kind, mortar_fine, mortar_coarse,
):
    k_high, k_low = mortar_tables()
    operands = (
        flow_state.transpose(1, 0, 2),
        cot_final.transpose(1, 0, 2),
        metric.reshape(1, LANES),
        send_col,
        send_row,
        exterior,
        face_kind,
        mortar_fine,
        mortar_coarse,
        jnp.asarray(stencil_tables()),
        jnp.asarray(k_high),
        jnp.asarray(k_low),
    )
    volume = pltpu.VMEM((1000, LANES), F32)
    out = pl.pallas_call(
        functools.partial(kernel, nr, nc),
        out_shape=jax.ShapeDtypeStruct((5, 125, LANES), F32),
        in_specs=[pl.BlockSpec(memory_space=pl.ANY)] * len(operands),
        out_specs=pl.BlockSpec(memory_space=pltpu.VMEM),
        scratch_shapes=[pltpu.VMEM(x.shape, x.dtype) for x in operands]
        + [volume] * 5
        + [
            pltpu.VMEM((4, 25, 8, WIDE), F32),
            pltpu.VMEM((4, 25, 8, WIDE), F32),
            pltpu.VMEM((25, 8, WIDE), F32),
            pltpu.VMEM((4, LANES, 768), F32),
            pltpu.VMEM((4, LANES, 8 * LANES), F32),
            pltpu.VMEM((LANES, LANES), F32),
            pltpu.VMEM((1, 5 * LANES), jnp.int32),
            pltpu.VMEM((5 * LANES, 2 * LANES), BF16),
            pltpu.VMEM((2 * LANES, 2 * LANES), BF16),
            pltpu.VMEM((8, LANES, LANES), BF16),
            pltpu.VMEM((8, WIDE), F32),
            pltpu.VMEM((4 * LANES, LANES), F32),
            pltpu.VMEM((4 * LANES, LANES), F32),
            pltpu.VMEM((4, COL_ROWS * nc + ROW_ROWS * nr, LANES), F32),
            pltpu.VMEM((4, COL_ROWS * nc + ROW_ROWS * nr, LANES), F32),
            pltpu.SemaphoreType.DMA((len(operands),)),
            pltpu.SemaphoreType.DMA((4,)),
            pltpu.SemaphoreType.DMA((4,)),
        ],
        compiler_params=pltpu.CompilerParams(
            collective_id=0, has_side_effects=True, vmem_limit_bytes=56 * 2**20
        ),
    )(*operands)
    return out.transpose(1, 0, 2)


def solution(mesh):
    both = ("row", "col")
    in_specs = (P(None, None, both), P(None, None, both), P(both)) + (P(both, None),) * 6
    return jax.shard_map(
        functools.partial(on_device, mesh.shape["row"], mesh.shape["col"]),
        mesh=mesh,
        in_specs=in_specs,
        out_specs=P(None, None, both),
        check_vma=False,
    )
```

```python
import functools
import math

import jax
import jax.numpy as jnp
import numpy as np
from jax import lax
from jax.experimental import pallas as pl
from jax.experimental.pallas import tpu as pltpu
from jax.sharding import PartitionSpec as P

STEP = 0.005
W_END = 0.1
COL_ROWS = 16
COL_SENT = 9
ROW_ROWS = 8
LANES = 128
GROUPS = 7
WIDE = GROUPS * LANES
MESH = pl.DeviceIdType.MESH
F32 = jnp.float32
BF16 = jnp.bfloat16
FIELD_ORDER = ((0, 1, 2, 3, 4), (0, 2, 1, 3, 4), (0, 3, 1, 2, 4))


def basis():
    inner = math.sqrt(3.0 / 7.0)
    x = np.array([-1.0, -inner, 0.0, inner, 1.0])
    w = np.array([0.1, 49.0 / 90.0, 32.0 / 45.0, 49.0 / 90.0, 0.1])

    def lagrange(at):
        out = np.ones((5, 5))
        for m in range(5):
            for n in range(5):
                if n != m:
                    out[:, m] *= (at - x[n]) / (x[m] - x[n])
        return out

    eye = np.eye(5)
    gaps = x[:, None] - x[None, :] + eye
    bary = 1.0 / np.prod(gaps, axis=1)
    diff = bary[None, :] / bary[:, None] / gaps * (1.0 - eye)
    diff = diff - eye * diff.sum(axis=1)[:, None]
    halves = [lagrange((x + 2.0 * a - 1.0) / 2.0) for a in (0, 1)]
    projs = [0.5 * (m.T * w[None, :]) / w[:, None] for m in halves]
    interp = [np.kron(halves[a], halves[b]) for a in (0, 1) for b in (0, 1)]
    project = [np.kron(projs[a], projs[b]) for a in (0, 1) for b in (0, 1)]
    return diff, interp, project


def stencil_tables():
    diff = basis()[0]
    parts = []
    for matrix in (diff, diff.T):
        along = np.zeros((5, 8))
        along[:, :5] = matrix.T
        parts.append(along.reshape(40))
        parts.append(np.repeat(matrix.reshape(25), 8))
    column = np.concatenate(parts)
    return np.repeat(column[:, None], LANES, axis=1).astype(np.float32)


def mortar_tables():
    _, interp, project = basis()
    out = np.zeros((4, 4, LANES, LANES))
    for q in range(4):
        for at, matrix in enumerate(
            (interp[q], project[q].T, project[q], interp[q].T)
        ):
            out[at, q, :125, :125] = np.kron(np.eye(5), matrix)
    out = out.reshape(4, 4 * LANES, LANES).astype(np.float32)
    high = out.astype(jnp.bfloat16)
    low = (out - high.astype(np.float32)).astype(jnp.bfloat16)
    return high, low


def split(x):
    high = x.astype(BF16)
    return high, (x - high.astype(F32)).astype(BF16)


def split_rows(x):
    return jnp.concatenate(split(x), axis=0)


def dot(a, b):
    return lax.dot_general(a, b, (((1,), (0,)), ((), ())), preferred_element_type=F32)


def dot_nt(a, b):
    return lax.dot_general(a, b, (((1,), (1,)), ((), ())), preferred_element_type=F32)


def pick(x, onehot):
    both = dot(split_rows(x), onehot)
    return both[: x.shape[0]] + both[x.shape[0] :]


def place(x, onehot):
    both = dot_nt(split_rows(x), onehot)
    return both[: x.shape[0]] + both[x.shape[0] :]


def col_offsets(nc):
    if nc != 32:
        return list(range(1, nc))
    every = [(y, x, c) for y in range(4) for x in range(4) for c in range(2)]
    return sorted(every[1:], key=lambda o: (-(2 - abs(o[0] - 2)) - (2 - abs(o[1] - 2)), o))


def col_peer(me, away, nc):
    if nc != 32:
        return lax.rem(me + away, nc)
    y, x, core = me // 8, lax.rem(me // 2, 4), lax.rem(me, 2)
    y, x, core = lax.rem(y + away[0], 4), lax.rem(x + away[1], 4), lax.rem(core + away[2], 2)
    return 8 * y + 2 * x + core


def rows_at(start, size=8):
    return pl.ds(pl.multiple_of(start, 8), size)


def kernel(
    nr, nc,
    u_hbm, c_hbm, met_hbm, col_hbm, row_hbm, ext_hbm, kind_hbm, fine_hbm, coarse_hbm,
    tab_hbm, khi_hbm, klo_hbm,
    out_hbm,
    un_ref, cn_ref, met_ref, col_ref, row_ref, exterior_ref, kind_ref, fine_ref, coarse_ref,
    tab_ref, khi_ref, klo_ref,
    u_ref, c_ref, u1_ref, acc_ref, fz_ref, own_ref, ext_ref, val_ref, tc_ref, xc_ref, vc_ref,
    term_ref, out_ref, list_ref, ohs_ref, ohr_ref, ohl_ref, lane_ref, slot_ref, came_ref,
    sbuf, rbuf, load_sem, send_sem, recv_sem, out_sem,
):
    mr = lax.axis_index("row")
    mc = lax.axis_index("col")
    loads = [
        pltpu.make_async_copy(src, dst, load_sem.at[n])
        for n, (src, dst) in enumerate(
            (
                (u_hbm, un_ref),
                (met_hbm, met_ref),
                (col_hbm, col_ref),
                (row_hbm, row_ref),
                (fine_hbm, fine_ref),
                (coarse_hbm, coarse_ref),
                (ext_hbm, exterior_ref),
                (kind_hbm, kind_ref),
                (c_hbm, cn_ref),
                (tab_hbm, tab_ref),
                (khi_hbm, khi_ref),
                (klo_hbm, klo_ref),
            )
        )
    ]
    for load in loads:
        load.start()
    barrier = pltpu.get_barrier_semaphore()

    def greet_col(k, carry):
        pl.semaphore_signal(
            barrier, inc=1, device_id=(mr, lax.rem(mc + k, nc)), device_id_type=MESH
        )
        return carry

    def greet_row(k, carry):
        pl.semaphore_signal(
            barrier, inc=1, device_id=(lax.rem(mr + k, nr), mc), device_id_type=MESH
        )
        return carry

    lax.fori_loop(1, nc, greet_col, 0)
    lax.fori_loop(1, nr, greet_row, 0)

    moved_rows = COL_SENT * (nc - 1) + ROW_ROWS * (nr - 1)
    row_base = COL_ROWS * nc


    for e in range(4):
        tc_ref[e, 120:128, :] = jnp.zeros((8, 768), F32)
    for load in loads[2:6]:
        load.wait()

    def natural(ref, wide_ref):
        for g in range(24):
            for f in range(5):
                at = 200 * f + 8 * g
                wide_ref[at : at + 8, :] = ref[f, 5 * g : 5 * g + 8, :]
        for f in range(5):
            at = 200 * f + 192
            wide_ref[at : at + 8, :] = jnp.ones((8, LANES), F32)
            wide_ref[at : at + 5, :] = ref[f, 120:125, :]

    def onehot(target, base=0):
        iota = lax.broadcasted_iota(jnp.int32, (LANES, LANES), 0) + base
        return jnp.where(iota == target, 1.0, 0.0).astype(BF16)

    list_ref[...] = jnp.full((1, 5 * LANES), 768, jnp.int32)
    list_ref[:, 0 : 5 * nc] = col_ref[...]
    list_ref[:, 2 * LANES : 2 * LANES + 4 * nc] = fine_ref[...]
    list_ref[:, 3 * LANES : 3 * LANES + 8 * nr] = row_ref[...]
    for q in range(4):
        list_ref[:, 4 * LANES + q * nc : 4 * LANES + (q + 1) * nc] = coarse_ref[...]

    def listed(n):
        return list_ref[:, n * LANES : (n + 1) * LANES]

    coarse_list = listed(4)
    for n, k in enumerate((0, 1, 5)):
        for half in range(2):
            ohs_ref[n * LANES : (n + 1) * LANES, half * LANES : (half + 1) * LANES] = onehot(
                listed(half), k * LANES
            )
    for n, k in enumerate((2, 3)):
        ohs_ref[(3 + n) * LANES : (4 + n) * LANES, 0:LANES] = onehot(listed(3), k * LANES)
    ohl_ref[6] = onehot(listed(2), 4 * LANES)
    ohl_ref[7] = onehot(coarse_list, 5 * LANES)

    loads[0].wait()
    natural(un_ref, u_ref)

    def receive_tables():
        vc_ref[120:128, :] = jnp.zeros((8, LANES), F32)
        came_ref[...] = jnp.zeros((4 * LANES, LANES), F32)
        loads[1].wait()
        loads[6].wait()
        loads[7].wait()
        for k in range(6):
            lanes = slice(k * LANES, (k + 1) * LANES)
            at = exterior_ref[:, lanes]
            near = (kind_ref[:, lanes] == 0) & (at < 768)
            ohl_ref[k] = onehot(jnp.where(near, at - (k ^ 1) * LANES, -1))
            far = (kind_ref[:, lanes] == 0) & (at >= 768)
            half = slice((k % 2) * LANES, (k % 2 + 1) * LANES)
            if k < 2:
                at = at - 768
                peer = (at * 205) >> 10
                at = (at - 5 * peer) * nc + peer
                ohr_ref[0:LANES, half] = onehot(jnp.where(far, at, -1))
            elif k < 4:
                ohr_ref[LANES:, half] = onehot(jnp.where(far, at - 768 - 5 * nc, -1))
        for k in range(GROUPS):
            lanes = slice(k * LANES, (k + 1) * LANES)
            one = jnp.ones((1, LANES), F32)
            if k < 6:
                kind = kind_ref[:, lanes]
                rows = [
                    one * (2.0 * (k % 2) - 1.0),
                    jnp.where(kind == 3, -1.0, 1.0),
                    one,
                    jnp.where((kind == 0) | (kind == 2), 1.0, 0.0),
                    jnp.where(kind == 1, 1.0, 0.0),
                    one,
                ]
            else:
                valid = jnp.where(coarse_list < 768, 1.0, 0.0)
                rows = [one, -one, -one, one, 0.0 * one, valid]
            for n, row in enumerate(rows):
                lane_ref[n : n + 1, lanes] = row


    def post(e, src_ref, scale):
        def take(a, carry):
            for k in range(6):
                d, h = k // 2, k % 2
                lanes = slice(k * LANES, (k + 1) * LANES)
                for f in range(5):
                    base = 200 * FIELD_ORDER[d][f]
                    if d == 0:
                        piece = src_ref[pl.ds(base + 40 * a + 4 * h, 5, 8), :]
                    elif d == 1:
                        piece = src_ref[rows_at(base + 40 * a + 32 * h), :]
                    else:
                        piece = src_ref[rows_at(base + 160 * h + 8 * a), :]
                    if scale is not None:
                        piece = piece * (met_ref[...] * (scale / W_END))
                    own_ref[e, 5 * f + a, : piece.shape[0], lanes] = piece
            return carry

        lax.fori_loop(0, 5, take, 0)
        for g in range(25):
            tc_ref[e, 5 * g : 5 * g + 5, :] = own_ref[e, g, 0:5, 0:768]
        both = split_rows(tc_ref[e])

        def group(k, count=1):
            return both[:, k * LANES : (k + count) * LANES]

        def listed_rows(at, x):
            x = x[:LANES] + x[LANES:]
            for n in range(x.shape[1] // LANES):
                slot_ref[at + n * LANES : at + (n + 1) * LANES, :] = x[:, n * LANES : (n + 1) * LANES].T

        listed_rows(0, dot(group(0, 2), ohs_ref[0:256, :]) + dot(group(5), ohs_ref[256:384, :]))
        listed_rows(2 * LANES, dot(group(4), ohl_ref[6]))
        listed_rows(3 * LANES, dot(group(2, 2), ohs_ref[384:640, 0:LANES]))
        for n in range(5):
            sbuf[e, pl.ds(n, nc, COL_ROWS), :] = slot_ref[pl.ds(n, nc, 5), :]
        for q in range(4):
            sbuf[e, pl.ds(5 + q, nc, COL_ROWS), :] = slot_ref[2 * LANES + q * nc : 2 * LANES + (q + 1) * nc, :]
        sbuf[e, row_base : row_base + ROW_ROWS * nr, :] = slot_ref[3 * LANES : 3 * LANES + ROW_ROWS * nr, :]
        if e == 0:
            pl.semaphore_wait(barrier, nc + nr - 2)

        for away in col_offsets(nc):
            peer = col_peer(mc, away, nc)
            pltpu.make_async_remote_copy(
                src_ref=sbuf.at[e, rows_at(COL_ROWS * peer, COL_SENT)],
                dst_ref=rbuf.at[e, rows_at(COL_ROWS * mc, COL_SENT)],
                send_sem=send_sem.at[e],
                recv_sem=recv_sem.at[e],
                device_id=(mr, peer),
                device_id_type=MESH,
            ).start()
        for away in sorted(range(1, nr), key=lambda k: -min(k, nr - k)):
            peer = lax.rem(mr + away, nr)
            pltpu.make_async_remote_copy(
                src_ref=sbuf.at[e, rows_at(row_base + ROW_ROWS * peer, ROW_ROWS)],
                dst_ref=rbuf.at[e, rows_at(row_base + ROW_ROWS * mr, ROW_ROWS)],
                send_sem=send_sem.at[e],
                recv_sem=recv_sem.at[e],
                device_id=(peer, mc),
                device_id_type=MESH,
            ).start()
        own_col = rows_at(COL_ROWS * mc, COL_ROWS)
        rbuf[e, own_col, :] = sbuf[e, own_col, :]
        own_row = rows_at(row_base + ROW_ROWS * mr, ROW_ROWS)
        rbuf[e, own_row, :] = sbuf[e, own_row, :]
    quarter = lax.broadcasted_iota(jnp.int32, (1, LANES), 1) // nc

    def by_quarter(at, x):
        hi, lo = split(x)
        k_hi, k_lo = khi_ref[at], klo_ref[at]
        full = dot(k_hi, hi) + (dot(k_lo, hi) + dot(k_hi, lo))
        total = jnp.where(quarter == 0, full[:LANES], 0.0)
        for q in range(1, 4):
            total = jnp.where(quarter == q, full[q * LANES : (q + 1) * LANES], total)
        return total

    def near(e, table):
        both = split_rows(tc_ref[e])

        def group(k):
            return both[:, k * LANES : (k + 1) * LANES]

        for k in range(6):
            got = dot(group(k ^ 1), ohl_ref[k])
            xc_ref[e, :, k * LANES : (k + 1) * LANES] = got[:LANES] + got[LANES:]
        got = dot(group(5), ohl_ref[7])
        xc_ref[e, :, 7 * LANES :] = by_quarter(table, got[:LANES] + got[LANES:])
        for g in range(25):
            own_ref[e, g, :, 6 * LANES :] = xc_ref[e, 5 * g : 5 * g + 8, WIDE:]

    def finish(e, table):
        size = pl.ds(0, moved_rows)
        whole = pltpu.make_async_copy(sbuf.at[e, size], rbuf.at[e, size], recv_sem.at[e])
        whole.wait()
        for n in range(4):
            came_ref[n * nc : (n + 1) * nc, :] = rbuf[e, pl.ds(n, nc, COL_ROWS), :]
        coarse = rbuf[e, pl.ds(4, nc, COL_ROWS), :]
        for q in range(4):
            came_ref[LANES + q * nc : LANES + (q + 1) * nc, :] = coarse
            came_ref[2 * LANES + q * nc : 2 * LANES + (q + 1) * nc, :] = rbuf[
                e, pl.ds(5 + q, nc, COL_ROWS), :
            ]
        came_ref[3 * LANES : 3 * LANES + ROW_ROWS * nr, :] = rbuf[e, row_base : row_base + ROW_ROWS * nr, :]
        for n, chunk in enumerate((0, 3)):
            got = pick(came_ref[chunk * LANES : (chunk + 1) * LANES, :].T, ohr_ref[n * LANES : (n + 1) * LANES, :])
            lanes = slice(2 * n * LANES, 2 * (n + 1) * LANES)
            xc_ref[e, :, lanes] = xc_ref[e, :, lanes] + got
        xc_ref[e, :, 6 * LANES : 7 * LANES] = came_ref[2 * LANES : 3 * LANES, :].T
        fine_side = by_quarter(table, came_ref[LANES : 2 * LANES, :].T)
        lanes = slice(4 * LANES, 5 * LANES)
        xc_ref[e, :, lanes] = xc_ref[e, :, lanes] + place(fine_side, ohl_ref[6])
        for g in range(25):
            ext_ref[e, g] = xc_ref[e, 5 * g : 5 * g + 8, 0:WIDE]

    def sent_all(e):
        size = pl.ds(0, moved_rows)
        pltpu.make_async_copy(sbuf.at[e, size], rbuf.at[e, size], send_sem.at[e]).wait()


    def lane_row(n):
        return lane_ref[n : n + 1, :]

    def both_states(e, a):
        own = [own_ref[e, 5 * f + a] for f in range(5)]
        ext = [ext_ref[e, 5 * f + a] for f in range(5)]
        return own, ext

    def fill_states(e, a):
        own, ext = both_states(e, a)
        gathered = lane_row(3) > 0.5
        valid = lane_row(5) > 0.5
        flip = 1.0 - 2.0 * lane_row(4)
        default = (1.0, 0.0, 0.0, 0.0, 1.0)
        own = [jnp.where(valid, own[f], default[f]) for f in range(5)]
        mirror = [own[f] * flip if f == 1 else own[f] for f in range(5)]
        ext = [jnp.where(gathered, ext[f], mirror[f]) for f in range(5)]
        ext = [jnp.where(valid, ext[f], default[f]) for f in range(5)]
        return own, ext

    def primitives(s):
        inv = 1.0 / s[0]
        vel = [s[1] * inv, s[2] * inv, s[3] * inv]
        square = vel[0] * vel[0] + vel[1] * vel[1] + vel[2] * vel[2]
        pressure = 0.4 * (s[4] - 0.5 * (s[1] * vel[0] + s[2] * vel[1] + s[3] * vel[2]))
        return inv, vel, square, pressure

    def face_flux(e):
        def body(a, carry):
            own, ext = fill_states(e, a)
            orient, sign = lane_row(0), lane_row(1)
            fluxes, parts = [], []
            for s in (own, ext):
                inv, vel, _, pressure = primitives(s)
                fluxes.append(
                    (
                        s[1],
                        s[1] * vel[0] + pressure,
                        s[2] * vel[0],
                        s[3] * vel[0],
                        (s[4] + pressure) * vel[0],
                    )
                )
                parts.append(vel[0] * vel[0] + 1.4 * pressure * inv)
            speed = jnp.sqrt(0.5 * (parts[0] + parts[1]))
            for f in range(5):
                val_ref[5 * f + a] = 0.5 * (
                    orient * (fluxes[0][f] - sign * fluxes[1][f])
                    + sign * speed * (ext[f] - own[f])
                )
            return carry

        lax.fori_loop(0, 5, body, 0)

    def terms_of(state, a):
        own, ext = fill_states(state, a)
        inv, vel, square, pressure = primitives(own)
        inv_b, vel_b, _, pressure_b = primitives(ext)
        sound = 1.4 * pressure * inv
        speed = jnp.sqrt(
            0.5 * (vel[0] * vel[0] + vel_b[0] * vel_b[0] + sound + 1.4 * pressure_b * inv_b)
        )
        return [
            *vel,
            (own[4] + pressure) * inv,
            0.2 * square,
            0.14 * square - vel[0] * vel[0] - 0.5 * sound,
            speed,
            0.5 * inv / speed,
            *[ext[f] - own[f] for f in range(5)],
        ]

    def face_terms(state):
        def body(a, carry):
            for n, term in enumerate(terms_of(state, a)):
                term_ref[n, a] = term
            return carry

        lax.fori_loop(0, 5, body, 0)

    def face_adjoint(state, cot):
        def body(a, carry):
            if state is None:
                terms = [term_ref[n, a] for n in range(13)]
            else:
                terms = terms_of(state, a)
            v_n, v_1, v_2, enthalpy, fifth, of_density, speed, half_over, *gap = terms
            y, y_ext = both_states(cot, a)
            gathered = lane_row(3) > 0.5
            flip = 1.0 - 2.0 * lane_row(4)
            y_ext = [
                jnp.where(gathered, y_ext[f], y[f] * flip if f == 1 else y[f]) for f in range(5)
            ]
            orient, sign = lane_row(0), lane_row(2)
            plus = [orient * (y_ext[f] + sign * y[f]) for f in range(5)]
            minus = [y[f] - y_ext[f] for f in range(5)]
            dots = minus[0] * gap[0]
            for f in range(1, 5):
                dots = dots + minus[f] * gap[f]
            spread = dots * half_over
            p_bar = plus[1] + plus[4] * v_n
            along = plus[1] * v_n + plus[2] * v_1 + plus[3] * v_2 + plus[4] * enthalpy
            side = 0.4 * p_bar + 0.28 * spread
            result = [
                fifth * p_bar - v_n * along + spread * of_density,
                v_n * (plus[1] - 0.4 * p_bar + 0.72 * spread) + plus[0] + along,
                v_n * plus[2] - v_1 * side,
                v_n * plus[3] - v_2 * side,
                plus[4] * v_n + side,
            ]
            for f in range(5):
                val_ref[5 * f + a] = 0.5 * (result[f] - speed * minus[f])
            return carry

        lax.fori_loop(0, 5, body, 0)

    def coarse_sum(table, factor):
        for g in range(25):
            vc_ref[5 * g : 5 * g + 5, :] = val_ref[g, 0:5, 6 * LANES :]
        back = place(by_quarter(table, vc_ref[...]), ohl_ref[7])
        vc_ref[...] = back
        for g in range(25):
            val_ref[g, :, 5 * LANES : 6 * LANES] = (
                val_ref[g, :, 5 * LANES : 6 * LANES] + factor * vc_ref[5 * g : 5 * g + 8, :]
            )
        vc_ref[120:128, :] = jnp.zeros((8, LANES), F32)

    def spread_faces(scale):
        def body(a, carry):
            for k in range(6):
                d, h = k // 2, k % 2
                lanes = slice(k * LANES, (k + 1) * LANES)
                for f in range(5):
                    base = 200 * FIELD_ORDER[d][f]
                    size = 5 if d == 0 else 8
                    piece = val_ref[5 * f + a, 0:size, lanes]
                    if scale is not None:
                        piece = piece * scale
                    if d == 0:
                        where = pl.ds(base + 40 * a + 4 * h, 5, 8)
                    elif d == 1:
                        where = rows_at(base + 40 * a + 32 * h)
                    else:
                        where = rows_at(base + 160 * h + 8 * a)
                    acc_ref[where, :] = acc_ref[where, :] + piece
            return carry

        lax.fori_loop(0, 5, body, 0)


    diff = basis()[0]

    def slab_along(x, transposed):
        base = 240 if transposed else 0
        total = None
        for m in range(5):
            term = tab_ref[base + 8 * m : base + 8 * m + 8, :] * x[:, m : m + 1, :]
            total = term if total is None else total + term
        return total

    def slab_across(x, transposed):
        matrix = diff.T if transposed else diff
        rows = []
        for k in range(5):
            total = float(matrix[k, 0]) * x[0]
            for m in range(1, 5):
                if matrix[k, m] != 0.0:
                    total = total + float(matrix[k, m]) * x[m]
            rows.append(total[None])
        return jnp.concatenate(rows, axis=0)

    def slab_stack(ref, f, level, transposed):
        base = 280 if transposed else 40
        total = None
        for m in range(5):
            coef = tab_ref[rows_at(base + 40 * level + 8 * m), :]
            term = coef[None] * slab(ref, f, m)
            total = term if total is None else total + term
        return total

    def slab(ref, f, level):
        return ref[rows_at(200 * f + 40 * level, 40), :].reshape(5, 8, LANES)

    def put(ref, f, level, x):
        ref[rows_at(200 * f + 40 * level, 40), :] = x.reshape(40, LANES)

    def volume_forward():
        def first(level, carry):
            s = [slab(u_ref, f, level) for f in range(5)]
            _, vel, _, pressure = primitives(s)
            total = s[4] + pressure

            def flux(d, f):
                if f == 0:
                    return s[d + 1]
                if f == 4:
                    return total * vel[d]
                term = s[f] * vel[d]
                return term + pressure if f == d + 1 else term

            for f in range(5):
                put(fz_ref, f, level, flux(2, f))
                put(
                    acc_ref, f, level,
                    slab_along(flux(0, f), False) + slab_across(flux(1, f), False),
                )
            return carry

        def second(level, carry):
            for f in range(5):
                total = slab(acc_ref, f, level) + slab_stack(fz_ref, f, level, False)
                put(acc_ref, f, level, total * (-met_ref[...])[None])
            return carry

        lax.fori_loop(0, 5, first, 0)
        lax.fori_loop(0, 5, second, 0)

    def volume_adjoint(state_ref, cot_ref, scale):
        def body(level, carry):
            s = [slab(state_ref, f, level) for f in range(5)]
            inv, vel, square, pressure = primitives(s)
            enthalpy = (s[4] + pressure) * inv
            factor = (met_ref[...] * (-scale))[None]
            out = [None] * 5
            p_sum = None
            extra = []

            def add(f, x):
                out[f] = x if out[f] is None else out[f] + x

            for d in range(3):
                w = []
                for f in range(5):
                    if d == 0:
                        w.append(slab_along(slab(cot_ref, f, level), True))
                    elif d == 1:
                        w.append(slab_across(slab(cot_ref, f, level), True))
                    else:
                        w.append(slab_stack(cot_ref, f, level, True))
                p_bar = w[d + 1] + w[4] * vel[d]
                p_sum = p_bar if p_sum is None else p_sum + p_bar
                along = w[1] * vel[0] + w[2] * vel[1] + w[3] * vel[2] + w[4] * enthalpy
                for k in range(3):
                    add(k + 1, vel[d] * w[k + 1])
                extra.append(w[0] + along)
                add(0, -vel[d] * along)
                add(4, w[4] * vel[d])
            add(0, 0.2 * square * p_sum)
            add(4, 0.4 * p_sum)
            for k in range(3):
                add(k + 1, extra[k] - 0.4 * vel[k] * p_sum)
            for f in range(5):
                put(acc_ref, f, level, out[f] * factor)
            return carry

        lax.fori_loop(0, 5, body, 0)


    post(0, u_ref, None)
    receive_tables()
    loads[8].wait()
    natural(cn_ref, c_ref)
    post(1, c_ref, 0.5 * STEP)
    for load in loads[9:]:
        load.wait()
    near(0, 0)
    volume_forward()
    finish(0, 0)
    face_flux(0)
    coarse_sum(2, -1.0)
    spread_faces(met_ref[...] * (1.0 / W_END))
    for f in range(5):
        at = slice(200 * f, 200 * f + 200)
        u1_ref[at, :] = u_ref[at, :] + STEP * acc_ref[at, :]
    post(2, u1_ref, None)
    near(2, 0)
    near(1, 1)
    finish(1, 1)
    volume_adjoint(u1_ref, c_ref, 0.5 * STEP)
    finish(2, 0)
    face_adjoint(2, 1)
    coarse_sum(3, 1.0)
    spread_faces(None)
    for f in range(5):
        at = slice(200 * f, 200 * f + 200)
        u1_ref[at, :] = 0.5 * c_ref[at, :] + acc_ref[at, :]
    post(3, u1_ref, STEP)
    near(3, 1)
    face_terms(0)
    volume_adjoint(u_ref, u1_ref, STEP)
    finish(3, 1)
    face_adjoint(None, 3)
    coarse_sum(3, 1.0)
    spread_faces(None)
    stores = []
    for f in range(5):
        for g in range(25):
            at = slice(200 * f + 8 * g, 200 * f + 8 * g + 5)
            out_ref[f, 5 * g : 5 * g + 5, :] = u1_ref[at, :] + acc_ref[at, :]
        stores.append(pltpu.make_async_copy(out_ref.at[f], out_hbm.at[f], out_sem.at[f]))
        stores[f].start()
    for e in range(4):
        sent_all(e)
    for store in stores:
        store.wait()


def on_device(
    nr, nc, flow_state, cot_final, metric,
    send_col, send_row, exterior, face_kind, mortar_fine, mortar_coarse,
):
    k_high, k_low = mortar_tables()
    operands = (
        flow_state.transpose(1, 0, 2),
        cot_final.transpose(1, 0, 2),
        metric.reshape(1, LANES),
        send_col,
        send_row,
        exterior,
        face_kind,
        mortar_fine,
        mortar_coarse,
        jnp.asarray(stencil_tables()),
        jnp.asarray(k_high),
        jnp.asarray(k_low),
    )
    volume = pltpu.VMEM((1000, LANES), F32)
    out = pl.pallas_call(
        functools.partial(kernel, nr, nc),
        out_shape=jax.ShapeDtypeStruct((5, 125, LANES), F32),
        in_specs=[pl.BlockSpec(memory_space=pl.ANY)] * len(operands),
        out_specs=pl.BlockSpec(memory_space=pl.ANY),
        scratch_shapes=[pltpu.VMEM(x.shape, x.dtype) for x in operands]
        + [volume] * 5
        + [
            pltpu.VMEM((4, 25, 8, WIDE), F32),
            pltpu.VMEM((4, 25, 8, WIDE), F32),
            pltpu.VMEM((25, 8, WIDE), F32),
            pltpu.VMEM((4, LANES, 768), F32),
            pltpu.VMEM((4, LANES, 8 * LANES), F32),
            pltpu.VMEM((LANES, LANES), F32),
            pltpu.VMEM((13, 5, 8, WIDE), F32),
            pltpu.VMEM((5, 125, LANES), F32),
            pltpu.VMEM((1, 5 * LANES), jnp.int32),
            pltpu.VMEM((5 * LANES, 2 * LANES), BF16),
            pltpu.VMEM((2 * LANES, 2 * LANES), BF16),
            pltpu.VMEM((8, LANES, LANES), BF16),
            pltpu.VMEM((8, WIDE), F32),
            pltpu.VMEM((4 * LANES, LANES), F32),
            pltpu.VMEM((4 * LANES, LANES), F32),
            pltpu.VMEM((4, COL_ROWS * nc + ROW_ROWS * nr, LANES), F32),
            pltpu.VMEM((4, COL_ROWS * nc + ROW_ROWS * nr, LANES), F32),
            pltpu.SemaphoreType.DMA((len(operands),)),
            pltpu.SemaphoreType.DMA((4,)),
            pltpu.SemaphoreType.DMA((4,)),
            pltpu.SemaphoreType.DMA((5,)),
        ],
        compiler_params=pltpu.CompilerParams(
            collective_id=0, has_side_effects=True, vmem_limit_bytes=56 * 2**20
        ),
    )(*operands)
    return 0.5 * cot_final + out.transpose(1, 0, 2)


def solution(mesh):
    both = ("row", "col")
    in_specs = (P(None, None, both), P(None, None, both), P(both)) + (P(both, None),) * 6
    return jax.shard_map(
        functools.partial(on_device, mesh.shape["row"], mesh.shape["col"]),
        mesh=mesh,
        in_specs=in_specs,
        out_specs=P(None, None, both),
        check_vma=False,
    )
```

```python
import functools
import math

import jax
import jax.numpy as jnp
import numpy as np
from jax import lax
from jax.experimental import pallas as pl
from jax.experimental.pallas import tpu as pltpu
from jax.sharding import PartitionSpec as P

STEP = 0.005
W_END = 0.1
COL_ROWS = 16
COL_SENT = 9
ROW_ROWS = 8
LANES = 128
GROUPS = 7
WIDE = GROUPS * LANES
MESH = pl.DeviceIdType.MESH
F32 = jnp.float32
BF16 = jnp.bfloat16
FIELD_ORDER = ((0, 1, 2, 3, 4), (0, 2, 1, 3, 4), (0, 3, 1, 2, 4))


def basis():
    inner = math.sqrt(3.0 / 7.0)
    x = np.array([-1.0, -inner, 0.0, inner, 1.0])
    w = np.array([0.1, 49.0 / 90.0, 32.0 / 45.0, 49.0 / 90.0, 0.1])

    def lagrange(at):
        out = np.ones((5, 5))
        for m in range(5):
            for n in range(5):
                if n != m:
                    out[:, m] *= (at - x[n]) / (x[m] - x[n])
        return out

    eye = np.eye(5)
    gaps = x[:, None] - x[None, :] + eye
    bary = 1.0 / np.prod(gaps, axis=1)
    diff = bary[None, :] / bary[:, None] / gaps * (1.0 - eye)
    diff = diff - eye * diff.sum(axis=1)[:, None]
    halves = [lagrange((x + 2.0 * a - 1.0) / 2.0) for a in (0, 1)]
    projs = [0.5 * (m.T * w[None, :]) / w[:, None] for m in halves]
    interp = [np.kron(halves[a], halves[b]) for a in (0, 1) for b in (0, 1)]
    project = [np.kron(projs[a], projs[b]) for a in (0, 1) for b in (0, 1)]
    return diff, interp, project


def stencil_tables():
    diff = basis()[0]
    parts = []
    for matrix in (diff, diff.T):
        along = np.zeros((5, 8))
        along[:, :5] = matrix.T
        parts.append(along.reshape(40))
        parts.append(np.repeat(matrix.reshape(25), 8))
    column = np.concatenate(parts)
    return np.repeat(column[:, None], LANES, axis=1).astype(np.float32)


def mortar_tables():
    _, interp, project = basis()
    out = np.zeros((4, 4, LANES, LANES))
    for q in range(4):
        for at, matrix in enumerate(
            (interp[q], project[q].T, project[q], interp[q].T)
        ):
            out[at, q, :125, :125] = np.kron(np.eye(5), matrix)
    out = out.reshape(4, 4 * LANES, LANES).astype(np.float32)
    high = out.astype(jnp.bfloat16)
    low = (out - high.astype(np.float32)).astype(jnp.bfloat16)
    return high, low


def split(x):
    high = x.astype(BF16)
    return high, (x - high.astype(F32)).astype(BF16)


def split_rows(x):
    return jnp.concatenate(split(x), axis=0)


def dot(a, b):
    return lax.dot_general(a, b, (((1,), (0,)), ((), ())), preferred_element_type=F32)


def dot_nt(a, b):
    return lax.dot_general(a, b, (((1,), (1,)), ((), ())), preferred_element_type=F32)


def pick(x, onehot):
    both = dot(split_rows(x), onehot)
    return both[: x.shape[0]] + both[x.shape[0] :]


def place(x, onehot):
    both = dot_nt(split_rows(x), onehot)
    return both[: x.shape[0]] + both[x.shape[0] :]


def col_offsets(nc):
    if nc != 32:
        return list(range(1, nc))
    every = [(y, x, c) for y in range(4) for x in range(4) for c in range(2)]
    return sorted(every[1:], key=lambda o: (-(2 - abs(o[0] - 2)) - (2 - abs(o[1] - 2)), o))


def col_peer(me, away, nc):
    if nc != 32:
        return lax.rem(me + away, nc)
    y, x, core = me // 8, lax.rem(me // 2, 4), lax.rem(me, 2)
    y, x, core = lax.rem(y + away[0], 4), lax.rem(x + away[1], 4), lax.rem(core + away[2], 2)
    return 8 * y + 2 * x + core


def rows_at(start, size=8):
    return pl.ds(pl.multiple_of(start, 8), size)


def kernel(
    nr, nc,
    u_hbm, c_hbm, met_hbm, col_hbm, row_hbm, ext_hbm, kind_hbm, fine_hbm, coarse_hbm,
    tab_hbm, khi_hbm, klo_hbm,
    out_hbm,
    un_ref, cn_ref, met_ref, col_ref, row_ref, exterior_ref, kind_ref, fine_ref, coarse_ref,
    tab_ref, khi_ref, klo_ref,
    u_ref, c_ref, u1_ref, acc_ref, fz_ref, own_ref, ext_ref, val_ref, tc_ref, xc_ref, vc_ref,
    term_ref, out_ref, list_ref, ohs_ref, ohr_ref, ohl_ref, lane_ref, slot_ref, came_ref,
    sbuf, rbuf, load_sem, send_sem, recv_sem, out_sem,
):
    mr = lax.axis_index("row")
    mc = lax.axis_index("col")
    loads = [
        pltpu.make_async_copy(src, dst, load_sem.at[n])
        for n, (src, dst) in enumerate(
            (
                (u_hbm, un_ref),
                (met_hbm, met_ref),
                (col_hbm, col_ref),
                (row_hbm, row_ref),
                (fine_hbm, fine_ref),
                (coarse_hbm, coarse_ref),
                (ext_hbm, exterior_ref),
                (kind_hbm, kind_ref),
                (c_hbm, cn_ref),
                (tab_hbm, tab_ref),
                (khi_hbm, khi_ref),
                (klo_hbm, klo_ref),
            )
        )
    ]
    for load in loads:
        load.start()
    barrier = pltpu.get_barrier_semaphore()

    def greet_col(k, carry):
        pl.semaphore_signal(
            barrier, inc=1, device_id=(mr, lax.rem(mc + k, nc)), device_id_type=MESH
        )
        return carry

    def greet_row(k, carry):
        pl.semaphore_signal(
            barrier, inc=1, device_id=(lax.rem(mr + k, nr), mc), device_id_type=MESH
        )
        return carry

    lax.fori_loop(1, nc, greet_col, 0)
    lax.fori_loop(1, nr, greet_row, 0)

    moved_rows = COL_SENT * (nc - 1) + ROW_ROWS * (nr - 1)
    row_base = COL_ROWS * nc


    for e in range(4):
        tc_ref[e, 120:128, :] = jnp.zeros((8, 768), F32)
    for load in loads[2:6]:
        load.wait()

    def natural(ref, wide_ref):
        for g in range(24):
            for f in range(5):
                at = 200 * f + 8 * g
                wide_ref[at : at + 8, :] = ref[f, 5 * g : 5 * g + 8, :]
        for f in range(5):
            at = 200 * f + 192
            wide_ref[at : at + 8, :] = jnp.ones((8, LANES), F32)
            wide_ref[at : at + 5, :] = ref[f, 120:125, :]

    def onehot(target, base=0):
        iota = lax.broadcasted_iota(jnp.int32, (LANES, LANES), 0) + base
        return jnp.where(iota == target, 1.0, 0.0).astype(BF16)

    list_ref[...] = jnp.full((1, 5 * LANES), 768, jnp.int32)
    list_ref[:, 0 : 5 * nc] = col_ref[...]
    list_ref[:, 2 * LANES : 2 * LANES + 4 * nc] = fine_ref[...]
    list_ref[:, 3 * LANES : 3 * LANES + 8 * nr] = row_ref[...]
    for q in range(4):
        list_ref[:, 4 * LANES + q * nc : 4 * LANES + (q + 1) * nc] = coarse_ref[...]

    def listed(n):
        return list_ref[:, n * LANES : (n + 1) * LANES]

    coarse_list = listed(4)
    for n, k in enumerate((0, 1, 5)):
        for half in range(2):
            ohs_ref[n * LANES : (n + 1) * LANES, half * LANES : (half + 1) * LANES] = onehot(
                listed(half), k * LANES
            )
    for n, k in enumerate((2, 3)):
        ohs_ref[(3 + n) * LANES : (4 + n) * LANES, 0:LANES] = onehot(listed(3), k * LANES)
    ohl_ref[6] = onehot(listed(2), 4 * LANES)
    ohl_ref[7] = onehot(coarse_list, 5 * LANES)

    loads[0].wait()
    natural(un_ref, u_ref)

    def receive_tables():
        vc_ref[120:128, :] = jnp.zeros((8, LANES), F32)
        came_ref[...] = jnp.zeros((4 * LANES, LANES), F32)
        loads[1].wait()
        loads[6].wait()
        loads[7].wait()
        for k in range(6):
            lanes = slice(k * LANES, (k + 1) * LANES)
            at = exterior_ref[:, lanes]
            near = (kind_ref[:, lanes] == 0) & (at < 768)
            ohl_ref[k] = onehot(jnp.where(near, at - (k ^ 1) * LANES, -1))
            far = (kind_ref[:, lanes] == 0) & (at >= 768)
            half = slice((k % 2) * LANES, (k % 2 + 1) * LANES)
            if k < 2:
                at = at - 768
                peer = (at * 205) >> 10
                at = (at - 5 * peer) * nc + peer
                ohr_ref[0:LANES, half] = onehot(jnp.where(far, at, -1))
            elif k < 4:
                ohr_ref[LANES:, half] = onehot(jnp.where(far, at - 768 - 5 * nc, -1))
        for k in range(GROUPS):
            lanes = slice(k * LANES, (k + 1) * LANES)
            one = jnp.ones((1, LANES), F32)
            if k < 6:
                kind = kind_ref[:, lanes]
                rows = [
                    one * (2.0 * (k % 2) - 1.0),
                    jnp.where(kind == 3, -1.0, 1.0),
                    one,
                    jnp.where((kind == 0) | (kind == 2), 1.0, 0.0),
                    jnp.where(kind == 1, 1.0, 0.0),
                    one,
                ]
            else:
                valid = jnp.where(coarse_list < 768, 1.0, 0.0)
                rows = [one, -one, -one, one, 0.0 * one, valid]
            for n, row in enumerate(rows):
                lane_ref[n : n + 1, lanes] = row


    def post(e, src_ref, scale):
        def take(a, carry):
            for k in range(6):
                d, h = k // 2, k % 2
                lanes = slice(k * LANES, (k + 1) * LANES)
                for f in range(5):
                    base = 200 * FIELD_ORDER[d][f]
                    if d == 0:
                        piece = src_ref[pl.ds(base + 40 * a + 4 * h, 5, 8), :]
                    elif d == 1:
                        piece = src_ref[rows_at(base + 40 * a + 32 * h), :]
                    else:
                        piece = src_ref[rows_at(base + 160 * h + 8 * a), :]
                    if scale is not None:
                        piece = piece * (met_ref[...] * (scale / W_END))
                    own_ref[e, 5 * f + a, : piece.shape[0], lanes] = piece
            return carry

        lax.fori_loop(0, 5, take, 0, unroll=True)
        for g in range(25):
            tc_ref[e, 5 * g : 5 * g + 5, :] = own_ref[e, g, 0:5, 0:768]
        both = split_rows(tc_ref[e])

        def group(k, count=1):
            return both[:, k * LANES : (k + count) * LANES]

        def listed_rows(at, x):
            x = x[:LANES] + x[LANES:]
            for n in range(x.shape[1] // LANES):
                slot_ref[at + n * LANES : at + (n + 1) * LANES, :] = x[:, n * LANES : (n + 1) * LANES].T

        listed_rows(0, dot(group(0, 2), ohs_ref[0:256, :]) + dot(group(5), ohs_ref[256:384, :]))
        listed_rows(2 * LANES, dot(group(4), ohl_ref[6]))
        listed_rows(3 * LANES, dot(group(2, 2), ohs_ref[384:640, 0:LANES]))
        for n in range(5):
            sbuf[e, pl.ds(n, nc, COL_ROWS), :] = slot_ref[pl.ds(n, nc, 5), :]
        for q in range(4):
            sbuf[e, pl.ds(5 + q, nc, COL_ROWS), :] = slot_ref[2 * LANES + q * nc : 2 * LANES + (q + 1) * nc, :]
        sbuf[e, row_base : row_base + ROW_ROWS * nr, :] = slot_ref[3 * LANES : 3 * LANES + ROW_ROWS * nr, :]
        if e == 0:
            pl.semaphore_wait(barrier, nc + nr - 2)

        for away in col_offsets(nc):
            peer = col_peer(mc, away, nc)
            pltpu.make_async_remote_copy(
                src_ref=sbuf.at[e, rows_at(COL_ROWS * peer, COL_SENT)],
                dst_ref=rbuf.at[e, rows_at(COL_ROWS * mc, COL_SENT)],
                send_sem=send_sem.at[e],
                recv_sem=recv_sem.at[e],
                device_id=(mr, peer),
                device_id_type=MESH,
            ).start()
        for away in sorted(range(1, nr), key=lambda k: -min(k, nr - k)):
            peer = lax.rem(mr + away, nr)
            pltpu.make_async_remote_copy(
                src_ref=sbuf.at[e, rows_at(row_base + ROW_ROWS * peer, ROW_ROWS)],
                dst_ref=rbuf.at[e, rows_at(row_base + ROW_ROWS * mr, ROW_ROWS)],
                send_sem=send_sem.at[e],
                recv_sem=recv_sem.at[e],
                device_id=(peer, mc),
                device_id_type=MESH,
            ).start()
        own_col = rows_at(COL_ROWS * mc, COL_ROWS)
        rbuf[e, own_col, :] = sbuf[e, own_col, :]
        own_row = rows_at(row_base + ROW_ROWS * mr, ROW_ROWS)
        rbuf[e, own_row, :] = sbuf[e, own_row, :]
    quarter = lax.broadcasted_iota(jnp.int32, (1, LANES), 1) // nc

    def by_quarter(at, x):
        hi, lo = split(x)
        k_hi, k_lo = khi_ref[at], klo_ref[at]
        full = dot(k_hi, hi) + (dot(k_lo, hi) + dot(k_hi, lo))
        total = jnp.where(quarter == 0, full[:LANES], 0.0)
        for q in range(1, 4):
            total = jnp.where(quarter == q, full[q * LANES : (q + 1) * LANES], total)
        return total

    def near(e, table):
        both = split_rows(tc_ref[e])

        def group(k):
            return both[:, k * LANES : (k + 1) * LANES]

        for k in range(6):
            got = dot(group(k ^ 1), ohl_ref[k])
            xc_ref[e, :, k * LANES : (k + 1) * LANES] = got[:LANES] + got[LANES:]
        got = dot(group(5), ohl_ref[7])
        xc_ref[e, :, 7 * LANES :] = by_quarter(table, got[:LANES] + got[LANES:])
        for g in range(25):
            own_ref[e, g, :, 6 * LANES :] = xc_ref[e, 5 * g : 5 * g + 8, WIDE:]

    def finish(e, table):
        size = pl.ds(0, moved_rows)
        whole = pltpu.make_async_copy(sbuf.at[e, size], rbuf.at[e, size], recv_sem.at[e])
        whole.wait()
        for n in range(4):
            came_ref[n * nc : (n + 1) * nc, :] = rbuf[e, pl.ds(n, nc, COL_ROWS), :]
        coarse = rbuf[e, pl.ds(4, nc, COL_ROWS), :]
        for q in range(4):
            came_ref[LANES + q * nc : LANES + (q + 1) * nc, :] = coarse
            came_ref[2 * LANES + q * nc : 2 * LANES + (q + 1) * nc, :] = rbuf[
                e, pl.ds(5 + q, nc, COL_ROWS), :
            ]
        came_ref[3 * LANES : 3 * LANES + ROW_ROWS * nr, :] = rbuf[e, row_base : row_base + ROW_ROWS * nr, :]
        for n, chunk in enumerate((0, 3)):
            got = pick(came_ref[chunk * LANES : (chunk + 1) * LANES, :].T, ohr_ref[n * LANES : (n + 1) * LANES, :])
            lanes = slice(2 * n * LANES, 2 * (n + 1) * LANES)
            xc_ref[e, :, lanes] = xc_ref[e, :, lanes] + got
        xc_ref[e, :, 6 * LANES : 7 * LANES] = came_ref[2 * LANES : 3 * LANES, :].T
        fine_side = by_quarter(table, came_ref[LANES : 2 * LANES, :].T)
        lanes = slice(4 * LANES, 5 * LANES)
        xc_ref[e, :, lanes] = xc_ref[e, :, lanes] + place(fine_side, ohl_ref[6])
        for g in range(25):
            ext_ref[e, g] = xc_ref[e, 5 * g : 5 * g + 8, 0:WIDE]

    def sent_all(e):
        size = pl.ds(0, moved_rows)
        pltpu.make_async_copy(sbuf.at[e, size], rbuf.at[e, size], send_sem.at[e]).wait()


    def lane_row(n):
        return lane_ref[n : n + 1, :]

    def both_states(e, a):
        own = [own_ref[e, 5 * f + a] for f in range(5)]
        ext = [ext_ref[e, 5 * f + a] for f in range(5)]
        return own, ext

    def fill_states(e, a):
        own, ext = both_states(e, a)
        gathered = lane_row(3) > 0.5
        valid = lane_row(5) > 0.5
        flip = 1.0 - 2.0 * lane_row(4)
        default = (1.0, 0.0, 0.0, 0.0, 1.0)
        own = [jnp.where(valid, own[f], default[f]) for f in range(5)]
        mirror = [own[f] * flip if f == 1 else own[f] for f in range(5)]
        ext = [jnp.where(gathered, ext[f], mirror[f]) for f in range(5)]
        ext = [jnp.where(valid, ext[f], default[f]) for f in range(5)]
        return own, ext

    def primitives(s):
        inv = 1.0 / s[0]
        vel = [s[1] * inv, s[2] * inv, s[3] * inv]
        square = vel[0] * vel[0] + vel[1] * vel[1] + vel[2] * vel[2]
        pressure = 0.4 * (s[4] - 0.5 * (s[1] * vel[0] + s[2] * vel[1] + s[3] * vel[2]))
        return inv, vel, square, pressure

    def face_flux(e):
        def body(a, carry):
            own, ext = fill_states(e, a)
            orient, sign = lane_row(0), lane_row(1)
            fluxes, parts = [], []
            for s in (own, ext):
                inv, vel, _, pressure = primitives(s)
                fluxes.append(
                    (
                        s[1],
                        s[1] * vel[0] + pressure,
                        s[2] * vel[0],
                        s[3] * vel[0],
                        (s[4] + pressure) * vel[0],
                    )
                )
                parts.append(vel[0] * vel[0] + 1.4 * pressure * inv)
            speed = jnp.sqrt(0.5 * (parts[0] + parts[1]))
            for f in range(5):
                val_ref[5 * f + a] = 0.5 * (
                    orient * (fluxes[0][f] - sign * fluxes[1][f])
                    + sign * speed * (ext[f] - own[f])
                )
            return carry

        lax.fori_loop(0, 5, body, 0, unroll=True)

    def terms_of(state, a):
        own, ext = fill_states(state, a)
        inv, vel, square, pressure = primitives(own)
        inv_b, vel_b, _, pressure_b = primitives(ext)
        sound = 1.4 * pressure * inv
        speed = jnp.sqrt(
            0.5 * (vel[0] * vel[0] + vel_b[0] * vel_b[0] + sound + 1.4 * pressure_b * inv_b)
        )
        return [
            *vel,
            (own[4] + pressure) * inv,
            0.2 * square,
            0.14 * square - vel[0] * vel[0] - 0.5 * sound,
            speed,
            0.5 * inv / speed,
            *[ext[f] - own[f] for f in range(5)],
        ]

    def face_terms(state):
        def body(a, carry):
            for n, term in enumerate(terms_of(state, a)):
                term_ref[n, a] = term
            return carry

        lax.fori_loop(0, 5, body, 0, unroll=True)

    def face_adjoint(state, cot):
        def body(a, carry):
            if state is None:
                terms = [term_ref[n, a] for n in range(13)]
            else:
                terms = terms_of(state, a)
            v_n, v_1, v_2, enthalpy, fifth, of_density, speed, half_over, *gap = terms
            y, y_ext = both_states(cot, a)
            gathered = lane_row(3) > 0.5
            flip = 1.0 - 2.0 * lane_row(4)
            y_ext = [
                jnp.where(gathered, y_ext[f], y[f] * flip if f == 1 else y[f]) for f in range(5)
            ]
            orient, sign = lane_row(0), lane_row(2)
            plus = [orient * (y_ext[f] + sign * y[f]) for f in range(5)]
            minus = [y[f] - y_ext[f] for f in range(5)]
            dots = minus[0] * gap[0]
            for f in range(1, 5):
                dots = dots + minus[f] * gap[f]
            spread = dots * half_over
            p_bar = plus[1] + plus[4] * v_n
            along = plus[1] * v_n + plus[2] * v_1 + plus[3] * v_2 + plus[4] * enthalpy
            side = 0.4 * p_bar + 0.28 * spread
            result = [
                fifth * p_bar - v_n * along + spread * of_density,
                v_n * (plus[1] - 0.4 * p_bar + 0.72 * spread) + plus[0] + along,
                v_n * plus[2] - v_1 * side,
                v_n * plus[3] - v_2 * side,
                plus[4] * v_n + side,
            ]
            for f in range(5):
                val_ref[5 * f + a] = 0.5 * (result[f] - speed * minus[f])
            return carry

        lax.fori_loop(0, 5, body, 0, unroll=True)

    def coarse_sum(table, factor):
        for g in range(25):
            vc_ref[5 * g : 5 * g + 5, :] = val_ref[g, 0:5, 6 * LANES :]
        back = place(by_quarter(table, vc_ref[...]), ohl_ref[7])
        vc_ref[...] = back
        for g in range(25):
            val_ref[g, :, 5 * LANES : 6 * LANES] = (
                val_ref[g, :, 5 * LANES : 6 * LANES] + factor * vc_ref[5 * g : 5 * g + 8, :]
            )
        vc_ref[120:128, :] = jnp.zeros((8, LANES), F32)

    def spread_faces(scale):
        def body(a, carry):
            for k in range(6):
                d, h = k // 2, k % 2
                lanes = slice(k * LANES, (k + 1) * LANES)
                for f in range(5):
                    base = 200 * FIELD_ORDER[d][f]
                    size = 5 if d == 0 else 8
                    piece = val_ref[5 * f + a, 0:size, lanes]
                    if scale is not None:
                        piece = piece * scale
                    if d == 0:
                        where = pl.ds(base + 40 * a + 4 * h, 5, 8)
                    elif d == 1:
                        where = rows_at(base + 40 * a + 32 * h)
                    else:
                        where = rows_at(base + 160 * h + 8 * a)
                    acc_ref[where, :] = acc_ref[where, :] + piece
            return carry

        lax.fori_loop(0, 5, body, 0, unroll=True)


    diff = basis()[0]

    def slab_along(x, transposed):
        base = 240 if transposed else 0
        total = None
        for m in range(5):
            term = tab_ref[base + 8 * m : base + 8 * m + 8, :] * x[:, m : m + 1, :]
            total = term if total is None else total + term
        return total

    def slab_across(x, transposed):
        matrix = diff.T if transposed else diff
        rows = []
        for k in range(5):
            total = float(matrix[k, 0]) * x[0]
            for m in range(1, 5):
                if matrix[k, m] != 0.0:
                    total = total + float(matrix[k, m]) * x[m]
            rows.append(total[None])
        return jnp.concatenate(rows, axis=0)

    def slab_stack(ref, f, level, transposed):
        base = 280 if transposed else 40
        total = None
        for m in range(5):
            coef = tab_ref[rows_at(base + 40 * level + 8 * m), :]
            term = coef[None] * slab(ref, f, m)
            total = term if total is None else total + term
        return total

    def slab(ref, f, level):
        return ref[rows_at(200 * f + 40 * level, 40), :].reshape(5, 8, LANES)

    def put(ref, f, level, x):
        ref[rows_at(200 * f + 40 * level, 40), :] = x.reshape(40, LANES)

    def volume_forward():
        def first(level, carry):
            s = [slab(u_ref, f, level) for f in range(5)]
            _, vel, _, pressure = primitives(s)
            total = s[4] + pressure

            def flux(d, f):
                if f == 0:
                    return s[d + 1]
                if f == 4:
                    return total * vel[d]
                term = s[f] * vel[d]
                return term + pressure if f == d + 1 else term

            for f in range(5):
                put(fz_ref, f, level, flux(2, f))
                put(
                    acc_ref, f, level,
                    slab_along(flux(0, f), False) + slab_across(flux(1, f), False),
                )
            return carry

        def second(level, carry):
            for f in range(5):
                total = slab(acc_ref, f, level) + slab_stack(fz_ref, f, level, False)
                put(acc_ref, f, level, total * (-met_ref[...])[None])
            return carry

        lax.fori_loop(0, 5, first, 0)
        lax.fori_loop(0, 5, second, 0)

    def volume_adjoint(state_ref, cot_ref, scale):
        def body(level, carry):
            s = [slab(state_ref, f, level) for f in range(5)]
            inv, vel, square, pressure = primitives(s)
            enthalpy = (s[4] + pressure) * inv
            factor = (met_ref[...] * (-scale))[None]
            out = [None] * 5
            p_sum = None
            extra = []

            def add(f, x):
                out[f] = x if out[f] is None else out[f] + x

            for d in range(3):
                w = []
                for f in range(5):
                    if d == 0:
                        w.append(slab_along(slab(cot_ref, f, level), True))
                    elif d == 1:
                        w.append(slab_across(slab(cot_ref, f, level), True))
                    else:
                        w.append(slab_stack(cot_ref, f, level, True))
                p_bar = w[d + 1] + w[4] * vel[d]
                p_sum = p_bar if p_sum is None else p_sum + p_bar
                along = w[1] * vel[0] + w[2] * vel[1] + w[3] * vel[2] + w[4] * enthalpy
                for k in range(3):
                    add(k + 1, vel[d] * w[k + 1])
                extra.append(w[0] + along)
                add(0, -vel[d] * along)
                add(4, w[4] * vel[d])
            add(0, 0.2 * square * p_sum)
            add(4, 0.4 * p_sum)
            for k in range(3):
                add(k + 1, extra[k] - 0.4 * vel[k] * p_sum)
            for f in range(5):
                put(acc_ref, f, level, out[f] * factor)
            return carry

        lax.fori_loop(0, 5, body, 0)


    post(0, u_ref, None)
    receive_tables()
    loads[8].wait()
    natural(cn_ref, c_ref)
    post(1, c_ref, 0.5 * STEP)
    for load in loads[9:]:
        load.wait()
    near(0, 0)
    volume_forward()
    finish(0, 0)
    face_flux(0)
    coarse_sum(2, -1.0)
    spread_faces(met_ref[...] * (1.0 / W_END))
    for f in range(5):
        at = slice(200 * f, 200 * f + 200)
        u1_ref[at, :] = u_ref[at, :] + STEP * acc_ref[at, :]
    post(2, u1_ref, None)
    near(2, 0)
    near(1, 1)
    finish(1, 1)
    volume_adjoint(u1_ref, c_ref, 0.5 * STEP)
    finish(2, 0)
    face_adjoint(2, 1)
    coarse_sum(3, 1.0)
    spread_faces(None)
    for f in range(5):
        at = slice(200 * f, 200 * f + 200)
        u1_ref[at, :] = 0.5 * c_ref[at, :] + acc_ref[at, :]
    post(3, u1_ref, STEP)
    near(3, 1)
    face_terms(0)
    volume_adjoint(u_ref, u1_ref, STEP)
    finish(3, 1)
    face_adjoint(None, 3)
    coarse_sum(3, 1.0)
    spread_faces(None)
    stores = []
    for f in range(5):
        for g in range(25):
            at = slice(200 * f + 8 * g, 200 * f + 8 * g + 5)
            out_ref[f, 5 * g : 5 * g + 5, :] = u1_ref[at, :] + acc_ref[at, :]
        stores.append(pltpu.make_async_copy(out_ref.at[f], out_hbm.at[f], out_sem.at[f]))
        stores[f].start()
    for e in range(4):
        sent_all(e)
    for store in stores:
        store.wait()


def on_device(
    nr, nc, flow_state, cot_final, metric,
    send_col, send_row, exterior, face_kind, mortar_fine, mortar_coarse,
):
    k_high, k_low = mortar_tables()
    operands = (
        flow_state.transpose(1, 0, 2),
        cot_final.transpose(1, 0, 2),
        metric.reshape(1, LANES),
        send_col,
        send_row,
        exterior,
        face_kind,
        mortar_fine,
        mortar_coarse,
        jnp.asarray(stencil_tables()),
        jnp.asarray(k_high),
        jnp.asarray(k_low),
    )
    volume = pltpu.VMEM((1000, LANES), F32)
    out = pl.pallas_call(
        functools.partial(kernel, nr, nc),
        out_shape=jax.ShapeDtypeStruct((5, 125, LANES), F32),
        in_specs=[pl.BlockSpec(memory_space=pl.ANY)] * len(operands),
        out_specs=pl.BlockSpec(memory_space=pl.ANY),
        scratch_shapes=[pltpu.VMEM(x.shape, x.dtype) for x in operands]
        + [volume] * 5
        + [
            pltpu.VMEM((4, 25, 8, WIDE), F32),
            pltpu.VMEM((4, 25, 8, WIDE), F32),
            pltpu.VMEM((25, 8, WIDE), F32),
            pltpu.VMEM((4, LANES, 768), F32),
            pltpu.VMEM((4, LANES, 8 * LANES), F32),
            pltpu.VMEM((LANES, LANES), F32),
            pltpu.VMEM((13, 5, 8, WIDE), F32),
            pltpu.VMEM((5, 125, LANES), F32),
            pltpu.VMEM((1, 5 * LANES), jnp.int32),
            pltpu.VMEM((5 * LANES, 2 * LANES), BF16),
            pltpu.VMEM((2 * LANES, 2 * LANES), BF16),
            pltpu.VMEM((8, LANES, LANES), BF16),
            pltpu.VMEM((8, WIDE), F32),
            pltpu.VMEM((4 * LANES, LANES), F32),
            pltpu.VMEM((4 * LANES, LANES), F32),
            pltpu.VMEM((4, COL_ROWS * nc + ROW_ROWS * nr, LANES), F32),
            pltpu.VMEM((4, COL_ROWS * nc + ROW_ROWS * nr, LANES), F32),
            pltpu.SemaphoreType.DMA((len(operands),)),
            pltpu.SemaphoreType.DMA((4,)),
            pltpu.SemaphoreType.DMA((4,)),
            pltpu.SemaphoreType.DMA((5,)),
        ],
        compiler_params=pltpu.CompilerParams(
            collective_id=0, has_side_effects=True, vmem_limit_bytes=56 * 2**20
        ),
    )(*operands)
    return 0.5 * cot_final + out.transpose(1, 0, 2)


def solution(mesh):
    both = ("row", "col")
    in_specs = (P(None, None, both), P(None, None, both), P(both)) + (P(both, None),) * 6
    return jax.shard_map(
        functools.partial(on_device, mesh.shape["row"], mesh.shape["col"]),
        mesh=mesh,
        in_specs=in_specs,
        out_specs=P(None, None, both),
        check_vma=False,
    )
```

```python
import functools
import math

import jax
import jax.numpy as jnp
import numpy as np
from jax import lax
from jax.experimental import pallas as pl
from jax.experimental.pallas import tpu as pltpu
from jax.sharding import PartitionSpec as P

STEP = 0.005
W_END = 0.1
COL_ROWS = 16
COL_SENT = 9
ROW_ROWS = 8
LANES = 128
GROUPS = 7
WIDE = GROUPS * LANES
MESH = pl.DeviceIdType.MESH
F32 = jnp.float32
BF16 = jnp.bfloat16
FIELD_ORDER = ((0, 1, 2, 3, 4), (0, 2, 1, 3, 4), (0, 3, 1, 2, 4))


def basis():
    inner = math.sqrt(3.0 / 7.0)
    x = np.array([-1.0, -inner, 0.0, inner, 1.0])
    w = np.array([0.1, 49.0 / 90.0, 32.0 / 45.0, 49.0 / 90.0, 0.1])

    def lagrange(at):
        out = np.ones((5, 5))
        for m in range(5):
            for n in range(5):
                if n != m:
                    out[:, m] *= (at - x[n]) / (x[m] - x[n])
        return out

    eye = np.eye(5)
    gaps = x[:, None] - x[None, :] + eye
    bary = 1.0 / np.prod(gaps, axis=1)
    diff = bary[None, :] / bary[:, None] / gaps * (1.0 - eye)
    diff = diff - eye * diff.sum(axis=1)[:, None]
    halves = [lagrange((x + 2.0 * a - 1.0) / 2.0) for a in (0, 1)]
    projs = [0.5 * (m.T * w[None, :]) / w[:, None] for m in halves]
    interp = [np.kron(halves[a], halves[b]) for a in (0, 1) for b in (0, 1)]
    project = [np.kron(projs[a], projs[b]) for a in (0, 1) for b in (0, 1)]
    return diff, interp, project


def stencil_tables():
    diff = basis()[0]
    parts = []
    for matrix in (diff, diff.T):
        along = np.zeros((5, 8))
        along[:, :5] = matrix.T
        parts.append(along.reshape(40))
        parts.append(np.repeat(matrix.reshape(25), 8))
    column = np.concatenate(parts)
    return np.repeat(column[:, None], LANES, axis=1).astype(np.float32)


def mortar_tables():
    _, interp, project = basis()
    out = np.zeros((4, 4, LANES, LANES))
    for q in range(4):
        for at, matrix in enumerate(
            (interp[q], project[q].T, project[q], interp[q].T)
        ):
            out[at, q, :125, :125] = np.kron(np.eye(5), matrix)
    out = out.reshape(4, 4 * LANES, LANES).astype(np.float32)
    high = out.astype(jnp.bfloat16)
    low = (out - high.astype(np.float32)).astype(jnp.bfloat16)
    return high, low


def split(x):
    high = x.astype(BF16)
    return high, (x - high.astype(F32)).astype(BF16)


def split_rows(x):
    return jnp.concatenate(split(x), axis=0)


def dot(a, b):
    return lax.dot_general(a, b, (((1,), (0,)), ((), ())), preferred_element_type=F32)


def dot_nt(a, b):
    return lax.dot_general(a, b, (((1,), (1,)), ((), ())), preferred_element_type=F32)


def pick(x, onehot):
    both = dot(split_rows(x), onehot)
    return both[: x.shape[0]] + both[x.shape[0] :]


def place(x, onehot):
    both = dot_nt(split_rows(x), onehot)
    return both[: x.shape[0]] + both[x.shape[0] :]


def col_offsets(nc):
    if nc != 32:
        return list(range(1, nc))
    every = [(y, x, c) for y in range(4) for x in range(4) for c in range(2)]
    return sorted(every[1:], key=lambda o: (-(2 - abs(o[0] - 2)) - (2 - abs(o[1] - 2)), o))


def row_offsets(nr):
    return sorted(range(1, nr), key=lambda k: -min(k, nr - k))


def col_peer(me, away, nc):
    if nc != 32:
        return lax.rem(me + away, nc)
    y, x, core = me // 8, lax.rem(me // 2, 4), lax.rem(me, 2)
    y, x, core = lax.rem(y + away[0], 4), lax.rem(x + away[1], 4), lax.rem(core + away[2], 2)
    return 8 * y + 2 * x + core


def rows_at(start, size=8):
    return pl.ds(pl.multiple_of(start, 8), size)


def kernel(
    nr, nc,
    u_hbm, c_hbm, met_hbm, col_hbm, row_hbm, ext_hbm, kind_hbm, fine_hbm, coarse_hbm,
    tab_hbm, khi_hbm, klo_hbm,
    out_hbm,
    un_ref, cn_ref, met_ref, col_ref, row_ref, exterior_ref, kind_ref, fine_ref, coarse_ref,
    tab_ref, khi_ref, klo_ref,
    u_ref, c_ref, u1_ref, acc_ref, fz_ref, own_ref, ext_ref, val_ref, tc_ref, xc_ref, vc_ref,
    term_ref, out_ref, list_ref, ohs_ref, ohr_ref, ohl_ref, lane_ref, slot_ref, came_ref,
    sbuf, rbuf, load_sem, send_sem, recv_sem, out_sem,
):
    mr = lax.axis_index("row")
    mc = lax.axis_index("col")
    barrier = pltpu.get_barrier_semaphore()
    for away in col_offsets(nc):
        pl.semaphore_signal(
            barrier, inc=1, device_id=(mr, col_peer(mc, away, nc)), device_id_type=MESH
        )
    for away in row_offsets(nr):
        pl.semaphore_signal(
            barrier, inc=1, device_id=(lax.rem(mr + away, nr), mc), device_id_type=MESH
        )
    loads = [
        pltpu.make_async_copy(src, dst, load_sem.at[n])
        for n, (src, dst) in enumerate(
            (
                (u_hbm, un_ref),
                (met_hbm, met_ref),
                (col_hbm, col_ref),
                (row_hbm, row_ref),
                (fine_hbm, fine_ref),
                (coarse_hbm, coarse_ref),
                (ext_hbm, exterior_ref),
                (kind_hbm, kind_ref),
                (c_hbm, cn_ref),
                (tab_hbm, tab_ref),
                (khi_hbm, khi_ref),
                (klo_hbm, klo_ref),
            )
        )
    ]
    for load in loads:
        load.start()
    moved_rows = COL_SENT * (nc - 1) + ROW_ROWS * (nr - 1)
    row_base = COL_ROWS * nc


    for e in range(4):
        tc_ref[e, 120:128, :] = jnp.zeros((8, 768), F32)
    for load in loads[2:6]:
        load.wait()

    def natural(ref, wide_ref):
        for g in range(24):
            for f in range(5):
                at = 200 * f + 8 * g
                wide_ref[at : at + 8, :] = ref[f, 5 * g : 5 * g + 8, :]
        for f in range(5):
            at = 200 * f + 192
            wide_ref[at : at + 8, :] = jnp.ones((8, LANES), F32)
            wide_ref[at : at + 5, :] = ref[f, 120:125, :]

    def onehot(target, base=0):
        iota = lax.broadcasted_iota(jnp.int32, (LANES, LANES), 0) + base
        return jnp.where(iota == target, 1.0, 0.0).astype(BF16)

    list_ref[...] = jnp.full((1, 5 * LANES), 768, jnp.int32)
    list_ref[:, 0 : 5 * nc] = col_ref[...]
    list_ref[:, 2 * LANES : 2 * LANES + 4 * nc] = fine_ref[...]
    list_ref[:, 3 * LANES : 3 * LANES + 8 * nr] = row_ref[...]
    for q in range(4):
        list_ref[:, 4 * LANES + q * nc : 4 * LANES + (q + 1) * nc] = coarse_ref[...]

    def listed(n):
        return list_ref[:, n * LANES : (n + 1) * LANES]

    coarse_list = listed(4)
    for n, k in enumerate((0, 1, 5)):
        for half in range(2):
            ohs_ref[n * LANES : (n + 1) * LANES, half * LANES : (half + 1) * LANES] = onehot(
                listed(half), k * LANES
            )
    for n, k in enumerate((2, 3)):
        ohs_ref[(3 + n) * LANES : (4 + n) * LANES, 0:LANES] = onehot(listed(3), k * LANES)
    ohl_ref[6] = onehot(listed(2), 4 * LANES)
    ohl_ref[7] = onehot(coarse_list, 5 * LANES)

    loads[0].wait()
    natural(un_ref, u_ref)

    def receive_tables():
        vc_ref[120:128, :] = jnp.zeros((8, LANES), F32)
        came_ref[...] = jnp.zeros((4 * LANES, LANES), F32)
        loads[1].wait()
        loads[6].wait()
        loads[7].wait()
        for k in range(6):
            lanes = slice(k * LANES, (k + 1) * LANES)
            at = exterior_ref[:, lanes]
            near = (kind_ref[:, lanes] == 0) & (at < 768)
            ohl_ref[k] = onehot(jnp.where(near, at - (k ^ 1) * LANES, -1))
            far = (kind_ref[:, lanes] == 0) & (at >= 768)
            half = slice((k % 2) * LANES, (k % 2 + 1) * LANES)
            if k < 2:
                at = at - 768
                peer = (at * 205) >> 10
                at = (at - 5 * peer) * nc + peer
                ohr_ref[0:LANES, half] = onehot(jnp.where(far, at, -1))
            elif k < 4:
                ohr_ref[LANES:, half] = onehot(jnp.where(far, at - 768 - 5 * nc, -1))
        for k in range(GROUPS):
            lanes = slice(k * LANES, (k + 1) * LANES)
            one = jnp.ones((1, LANES), F32)
            if k < 6:
                kind = kind_ref[:, lanes]
                rows = [
                    one * (2.0 * (k % 2) - 1.0),
                    jnp.where(kind == 3, -1.0, 1.0),
                    one,
                    jnp.where((kind == 0) | (kind == 2), 1.0, 0.0),
                    jnp.where(kind == 1, 1.0, 0.0),
                    one,
                ]
            else:
                valid = jnp.where(coarse_list < 768, 1.0, 0.0)
                rows = [one, -one, -one, one, 0.0 * one, valid]
            for n, row in enumerate(rows):
                lane_ref[n : n + 1, lanes] = row


    def post(e, src_ref, scale):
        def take(a, carry):
            for k in range(6):
                d, h = k // 2, k % 2
                lanes = slice(k * LANES, (k + 1) * LANES)
                for f in range(5):
                    base = 200 * FIELD_ORDER[d][f]
                    if d == 0:
                        piece = src_ref[pl.ds(base + 40 * a + 4 * h, 5, 8), :]
                    elif d == 1:
                        piece = src_ref[rows_at(base + 40 * a + 32 * h), :]
                    else:
                        piece = src_ref[rows_at(base + 160 * h + 8 * a), :]
                    if scale is not None:
                        piece = piece * (met_ref[...] * (scale / W_END))
                    own_ref[e, 5 * f + a, : piece.shape[0], lanes] = piece
            return carry

        lax.fori_loop(0, 5, take, 0, unroll=True)
        for g in range(25):
            tc_ref[e, 5 * g : 5 * g + 5, :] = own_ref[e, g, 0:5, 0:768]
        both = split_rows(tc_ref[e])

        def group(k, count=1):
            return both[:, k * LANES : (k + count) * LANES]

        def listed_rows(at, x):
            x = x[:LANES] + x[LANES:]
            for n in range(x.shape[1] // LANES):
                slot_ref[at + n * LANES : at + (n + 1) * LANES, :] = x[:, n * LANES : (n + 1) * LANES].T

        listed_rows(0, dot(group(0, 2), ohs_ref[0:256, :]) + dot(group(5), ohs_ref[256:384, :]))
        listed_rows(2 * LANES, dot(group(4), ohl_ref[6]))
        listed_rows(3 * LANES, dot(group(2, 2), ohs_ref[384:640, 0:LANES]))
        for n in range(5):
            sbuf[e, pl.ds(n, nc, COL_ROWS), :] = slot_ref[pl.ds(n, nc, 5), :]
        for q in range(4):
            sbuf[e, pl.ds(5 + q, nc, COL_ROWS), :] = slot_ref[2 * LANES + q * nc : 2 * LANES + (q + 1) * nc, :]
        sbuf[e, row_base : row_base + ROW_ROWS * nr, :] = slot_ref[3 * LANES : 3 * LANES + ROW_ROWS * nr, :]
        if e == 0:
            pl.semaphore_wait(barrier, nc + nr - 2)

        for away in col_offsets(nc):
            peer = col_peer(mc, away, nc)
            pltpu.make_async_remote_copy(
                src_ref=sbuf.at[e, rows_at(COL_ROWS * peer, COL_SENT)],
                dst_ref=rbuf.at[e, rows_at(COL_ROWS * mc, COL_SENT)],
                send_sem=send_sem.at[e],
                recv_sem=recv_sem.at[e],
                device_id=(mr, peer),
                device_id_type=MESH,
            ).start()
        for away in row_offsets(nr):
            peer = lax.rem(mr + away, nr)
            pltpu.make_async_remote_copy(
                src_ref=sbuf.at[e, rows_at(row_base + ROW_ROWS * peer, ROW_ROWS)],
                dst_ref=rbuf.at[e, rows_at(row_base + ROW_ROWS * mr, ROW_ROWS)],
                send_sem=send_sem.at[e],
                recv_sem=recv_sem.at[e],
                device_id=(peer, mc),
                device_id_type=MESH,
            ).start()
        own_col = rows_at(COL_ROWS * mc, COL_ROWS)
        rbuf[e, own_col, :] = sbuf[e, own_col, :]
        own_row = rows_at(row_base + ROW_ROWS * mr, ROW_ROWS)
        rbuf[e, own_row, :] = sbuf[e, own_row, :]
    quarter = lax.broadcasted_iota(jnp.int32, (1, LANES), 1) // nc

    def by_quarter(at, x):
        hi, lo = split(x)
        k_hi, k_lo = khi_ref[at], klo_ref[at]
        full = dot(k_hi, hi) + (dot(k_lo, hi) + dot(k_hi, lo))
        total = jnp.where(quarter == 0, full[:LANES], 0.0)
        for q in range(1, 4):
            total = jnp.where(quarter == q, full[q * LANES : (q + 1) * LANES], total)
        return total

    def near(e, table):
        both = split_rows(tc_ref[e])

        def group(k):
            return both[:, k * LANES : (k + 1) * LANES]

        for k in range(6):
            got = dot(group(k ^ 1), ohl_ref[k])
            xc_ref[e, :, k * LANES : (k + 1) * LANES] = got[:LANES] + got[LANES:]
        got = dot(group(5), ohl_ref[7])
        xc_ref[e, :, 7 * LANES :] = by_quarter(table, got[:LANES] + got[LANES:])
        for g in range(25):
            own_ref[e, g, :, 6 * LANES :] = xc_ref[e, 5 * g : 5 * g + 8, WIDE:]

    def finish(e, table):
        size = pl.ds(0, moved_rows)
        whole = pltpu.make_async_copy(sbuf.at[e, size], rbuf.at[e, size], recv_sem.at[e])
        whole.wait()
        for n in range(4):
            came_ref[n * nc : (n + 1) * nc, :] = rbuf[e, pl.ds(n, nc, COL_ROWS), :]
        coarse = rbuf[e, pl.ds(4, nc, COL_ROWS), :]
        for q in range(4):
            came_ref[LANES + q * nc : LANES + (q + 1) * nc, :] = coarse
            came_ref[2 * LANES + q * nc : 2 * LANES + (q + 1) * nc, :] = rbuf[
                e, pl.ds(5 + q, nc, COL_ROWS), :
            ]
        came_ref[3 * LANES : 3 * LANES + ROW_ROWS * nr, :] = rbuf[e, row_base : row_base + ROW_ROWS * nr, :]
        for n, chunk in enumerate((0, 3)):
            got = pick(came_ref[chunk * LANES : (chunk + 1) * LANES, :].T, ohr_ref[n * LANES : (n + 1) * LANES, :])
            lanes = slice(2 * n * LANES, 2 * (n + 1) * LANES)
            xc_ref[e, :, lanes] = xc_ref[e, :, lanes] + got
        xc_ref[e, :, 6 * LANES : 7 * LANES] = came_ref[2 * LANES : 3 * LANES, :].T
        fine_side = by_quarter(table, came_ref[LANES : 2 * LANES, :].T)
        lanes = slice(4 * LANES, 5 * LANES)
        xc_ref[e, :, lanes] = xc_ref[e, :, lanes] + place(fine_side, ohl_ref[6])
        for g in range(25):
            ext_ref[e, g] = xc_ref[e, 5 * g : 5 * g + 8, 0:WIDE]

    def sent_all(e):
        size = pl.ds(0, moved_rows)
        pltpu.make_async_copy(sbuf.at[e, size], rbuf.at[e, size], send_sem.at[e]).wait()


    def lane_row(n):
        return lane_ref[n : n + 1, :]

    def both_states(e, a):
        own = [own_ref[e, 5 * f + a] for f in range(5)]
        ext = [ext_ref[e, 5 * f + a] for f in range(5)]
        return own, ext

    def fill_states(e, a):
        own, ext = both_states(e, a)
        gathered = lane_row(3) > 0.5
        valid = lane_row(5) > 0.5
        flip = 1.0 - 2.0 * lane_row(4)
        default = (1.0, 0.0, 0.0, 0.0, 1.0)
        own = [jnp.where(valid, own[f], default[f]) for f in range(5)]
        mirror = [own[f] * flip if f == 1 else own[f] for f in range(5)]
        ext = [jnp.where(gathered, ext[f], mirror[f]) for f in range(5)]
        ext = [jnp.where(valid, ext[f], default[f]) for f in range(5)]
        return own, ext

    def primitives(s):
        inv = 1.0 / s[0]
        vel = [s[1] * inv, s[2] * inv, s[3] * inv]
        square = vel[0] * vel[0] + vel[1] * vel[1] + vel[2] * vel[2]
        pressure = 0.4 * (s[4] - 0.5 * (s[1] * vel[0] + s[2] * vel[1] + s[3] * vel[2]))
        return inv, vel, square, pressure

    def face_flux(e):
        def body(a, carry):
            own, ext = fill_states(e, a)
            orient, sign = lane_row(0), lane_row(1)
            fluxes, parts = [], []
            for s in (own, ext):
                inv, vel, _, pressure = primitives(s)
                fluxes.append(
                    (
                        s[1],
                        s[1] * vel[0] + pressure,
                        s[2] * vel[0],
                        s[3] * vel[0],
                        (s[4] + pressure) * vel[0],
                    )
                )
                parts.append(vel[0] * vel[0] + 1.4 * pressure * inv)
            speed = jnp.sqrt(0.5 * (parts[0] + parts[1]))
            for f in range(5):
                val_ref[5 * f + a] = 0.5 * (
                    orient * (fluxes[0][f] - sign * fluxes[1][f])
                    + sign * speed * (ext[f] - own[f])
                )
            return carry

        lax.fori_loop(0, 5, body, 0, unroll=True)

    def terms_of(state, a):
        own, ext = fill_states(state, a)
        inv, vel, square, pressure = primitives(own)
        inv_b, vel_b, _, pressure_b = primitives(ext)
        sound = 1.4 * pressure * inv
        speed = jnp.sqrt(
            0.5 * (vel[0] * vel[0] + vel_b[0] * vel_b[0] + sound + 1.4 * pressure_b * inv_b)
        )
        return [
            *vel,
            (own[4] + pressure) * inv,
            0.2 * square,
            0.14 * square - vel[0] * vel[0] - 0.5 * sound,
            speed,
            0.5 * inv / speed,
            *[ext[f] - own[f] for f in range(5)],
        ]

    def face_terms(state):
        def body(a, carry):
            for n, term in enumerate(terms_of(state, a)):
                term_ref[n, a] = term
            return carry

        lax.fori_loop(0, 5, body, 0, unroll=True)

    def face_adjoint(state, cot):
        def body(a, carry):
            if state is None:
                terms = [term_ref[n, a] for n in range(13)]
            else:
                terms = terms_of(state, a)
            v_n, v_1, v_2, enthalpy, fifth, of_density, speed, half_over, *gap = terms
            y, y_ext = both_states(cot, a)
            gathered = lane_row(3) > 0.5
            flip = 1.0 - 2.0 * lane_row(4)
            y_ext = [
                jnp.where(gathered, y_ext[f], y[f] * flip if f == 1 else y[f]) for f in range(5)
            ]
            orient, sign = lane_row(0), lane_row(2)
            plus = [orient * (y_ext[f] + sign * y[f]) for f in range(5)]
            minus = [y[f] - y_ext[f] for f in range(5)]
            dots = minus[0] * gap[0]
            for f in range(1, 5):
                dots = dots + minus[f] * gap[f]
            spread = dots * half_over
            p_bar = plus[1] + plus[4] * v_n
            along = plus[1] * v_n + plus[2] * v_1 + plus[3] * v_2 + plus[4] * enthalpy
            side = 0.4 * p_bar + 0.28 * spread
            result = [
                fifth * p_bar - v_n * along + spread * of_density,
                v_n * (plus[1] - 0.4 * p_bar + 0.72 * spread) + plus[0] + along,
                v_n * plus[2] - v_1 * side,
                v_n * plus[3] - v_2 * side,
                plus[4] * v_n + side,
            ]
            for f in range(5):
                val_ref[5 * f + a] = 0.5 * (result[f] - speed * minus[f])
            return carry

        lax.fori_loop(0, 5, body, 0, unroll=True)

    def coarse_sum(table, factor):
        for g in range(25):
            vc_ref[5 * g : 5 * g + 5, :] = val_ref[g, 0:5, 6 * LANES :]
        back = place(by_quarter(table, vc_ref[...]), ohl_ref[7])
        vc_ref[...] = back
        for g in range(25):
            val_ref[g, :, 5 * LANES : 6 * LANES] = (
                val_ref[g, :, 5 * LANES : 6 * LANES] + factor * vc_ref[5 * g : 5 * g + 8, :]
            )
        vc_ref[120:128, :] = jnp.zeros((8, LANES), F32)

    def spread_faces(scale):
        def body(a, carry):
            for k in range(6):
                d, h = k // 2, k % 2
                lanes = slice(k * LANES, (k + 1) * LANES)
                for f in range(5):
                    base = 200 * FIELD_ORDER[d][f]
                    size = 5 if d == 0 else 8
                    piece = val_ref[5 * f + a, 0:size, lanes]
                    if scale is not None:
                        piece = piece * scale
                    if d == 0:
                        where = pl.ds(base + 40 * a + 4 * h, 5, 8)
                    elif d == 1:
                        where = rows_at(base + 40 * a + 32 * h)
                    else:
                        where = rows_at(base + 160 * h + 8 * a)
                    acc_ref[where, :] = acc_ref[where, :] + piece
            return carry

        lax.fori_loop(0, 5, body, 0, unroll=True)


    diff = basis()[0]

    def slab_along(x, transposed):
        base = 240 if transposed else 0
        total = None
        for m in range(5):
            term = tab_ref[base + 8 * m : base + 8 * m + 8, :] * x[:, m : m + 1, :]
            total = term if total is None else total + term
        return total

    def slab_across(x, transposed):
        matrix = diff.T if transposed else diff
        rows = []
        for k in range(5):
            total = float(matrix[k, 0]) * x[0]
            for m in range(1, 5):
                if matrix[k, m] != 0.0:
                    total = total + float(matrix[k, m]) * x[m]
            rows.append(total[None])
        return jnp.concatenate(rows, axis=0)

    def slab_stack(ref, f, level, transposed):
        base = 280 if transposed else 40
        total = None
        for m in range(5):
            coef = tab_ref[rows_at(base + 40 * level + 8 * m), :]
            term = coef[None] * slab(ref, f, m)
            total = term if total is None else total + term
        return total

    def slab(ref, f, level):
        return ref[rows_at(200 * f + 40 * level, 40), :].reshape(5, 8, LANES)

    def put(ref, f, level, x):
        ref[rows_at(200 * f + 40 * level, 40), :] = x.reshape(40, LANES)

    def volume_forward():
        def first(level, carry):
            s = [slab(u_ref, f, level) for f in range(5)]
            _, vel, _, pressure = primitives(s)
            total = s[4] + pressure

            def flux(d, f):
                if f == 0:
                    return s[d + 1]
                if f == 4:
                    return total * vel[d]
                term = s[f] * vel[d]
                return term + pressure if f == d + 1 else term

            for f in range(5):
                put(fz_ref, f, level, flux(2, f))
                put(
                    acc_ref, f, level,
                    slab_along(flux(0, f), False) + slab_across(flux(1, f), False),
                )
            return carry

        def second(level, carry):
            for f in range(5):
                total = slab(acc_ref, f, level) + slab_stack(fz_ref, f, level, False)
                put(acc_ref, f, level, total * (-met_ref[...])[None])
            return carry

        lax.fori_loop(0, 5, first, 0)
        lax.fori_loop(0, 5, second, 0)

    def volume_adjoint(state_ref, cot_ref, scale):
        def body(level, carry):
            s = [slab(state_ref, f, level) for f in range(5)]
            inv, vel, square, pressure = primitives(s)
            enthalpy = (s[4] + pressure) * inv
            factor = (met_ref[...] * (-scale))[None]
            out = [None] * 5
            p_sum = None
            extra = []

            def add(f, x):
                out[f] = x if out[f] is None else out[f] + x

            for d in range(3):
                w = []
                for f in range(5):
                    if d == 0:
                        w.append(slab_along(slab(cot_ref, f, level), True))
                    elif d == 1:
                        w.append(slab_across(slab(cot_ref, f, level), True))
                    else:
                        w.append(slab_stack(cot_ref, f, level, True))
                p_bar = w[d + 1] + w[4] * vel[d]
                p_sum = p_bar if p_sum is None else p_sum + p_bar
                along = w[1] * vel[0] + w[2] * vel[1] + w[3] * vel[2] + w[4] * enthalpy
                for k in range(3):
                    add(k + 1, vel[d] * w[k + 1])
                extra.append(w[0] + along)
                add(0, -vel[d] * along)
                add(4, w[4] * vel[d])
            add(0, 0.2 * square * p_sum)
            add(4, 0.4 * p_sum)
            for k in range(3):
                add(k + 1, extra[k] - 0.4 * vel[k] * p_sum)
            for f in range(5):
                put(acc_ref, f, level, out[f] * factor)
            return carry

        lax.fori_loop(0, 5, body, 0)


    post(0, u_ref, None)
    receive_tables()
    loads[8].wait()
    natural(cn_ref, c_ref)
    post(1, c_ref, 0.5 * STEP)
    for load in loads[9:]:
        load.wait()
    near(0, 0)
    volume_forward()
    finish(0, 0)
    face_flux(0)
    coarse_sum(2, -1.0)
    spread_faces(met_ref[...] * (1.0 / W_END))
    for f in range(5):
        at = slice(200 * f, 200 * f + 200)
        u1_ref[at, :] = u_ref[at, :] + STEP * acc_ref[at, :]
    post(2, u1_ref, None)
    near(2, 0)
    near(1, 1)
    finish(1, 1)
    volume_adjoint(u1_ref, c_ref, 0.5 * STEP)
    finish(2, 0)
    face_adjoint(2, 1)
    coarse_sum(3, 1.0)
    spread_faces(None)
    for f in range(5):
        at = slice(200 * f, 200 * f + 200)
        u1_ref[at, :] = 0.5 * c_ref[at, :] + acc_ref[at, :]
    post(3, u1_ref, STEP)
    near(3, 1)
    face_terms(0)
    volume_adjoint(u_ref, u1_ref, STEP)
    finish(3, 1)
    face_adjoint(None, 3)
    coarse_sum(3, 1.0)
    spread_faces(None)
    stores = []
    for f in range(5):
        for g in range(25):
            at = slice(200 * f + 8 * g, 200 * f + 8 * g + 5)
            out_ref[f, 5 * g : 5 * g + 5, :] = u1_ref[at, :] + acc_ref[at, :]
        stores.append(pltpu.make_async_copy(out_ref.at[f], out_hbm.at[f], out_sem.at[f]))
        stores[f].start()
    for e in range(4):
        sent_all(e)
    for store in stores:
        store.wait()


def on_device(
    nr, nc, flow_state, cot_final, metric,
    send_col, send_row, exterior, face_kind, mortar_fine, mortar_coarse,
):
    k_high, k_low = mortar_tables()
    operands = (
        flow_state.transpose(1, 0, 2),
        cot_final.transpose(1, 0, 2),
        metric.reshape(1, LANES),
        send_col,
        send_row,
        exterior,
        face_kind,
        mortar_fine,
        mortar_coarse,
        jnp.asarray(stencil_tables()),
        jnp.asarray(k_high),
        jnp.asarray(k_low),
    )
    volume = pltpu.VMEM((1000, LANES), F32)
    out = pl.pallas_call(
        functools.partial(kernel, nr, nc),
        out_shape=jax.ShapeDtypeStruct((5, 125, LANES), F32),
        in_specs=[pl.BlockSpec(memory_space=pl.ANY)] * len(operands),
        out_specs=pl.BlockSpec(memory_space=pl.ANY),
        scratch_shapes=[pltpu.VMEM(x.shape, x.dtype) for x in operands]
        + [volume] * 5
        + [
            pltpu.VMEM((4, 25, 8, WIDE), F32),
            pltpu.VMEM((4, 25, 8, WIDE), F32),
            pltpu.VMEM((25, 8, WIDE), F32),
            pltpu.VMEM((4, LANES, 768), F32),
            pltpu.VMEM((4, LANES, 8 * LANES), F32),
            pltpu.VMEM((LANES, LANES), F32),
            pltpu.VMEM((13, 5, 8, WIDE), F32),
            pltpu.VMEM((5, 125, LANES), F32),
            pltpu.VMEM((1, 5 * LANES), jnp.int32),
            pltpu.VMEM((5 * LANES, 2 * LANES), BF16),
            pltpu.VMEM((2 * LANES, 2 * LANES), BF16),
            pltpu.VMEM((8, LANES, LANES), BF16),
            pltpu.VMEM((8, WIDE), F32),
            pltpu.VMEM((4 * LANES, LANES), F32),
            pltpu.VMEM((4 * LANES, LANES), F32),
            pltpu.VMEM((4, COL_ROWS * nc + ROW_ROWS * nr, LANES), F32),
            pltpu.VMEM((4, COL_ROWS * nc + ROW_ROWS * nr, LANES), F32),
            pltpu.SemaphoreType.DMA((len(operands),)),
            pltpu.SemaphoreType.DMA((4,)),
            pltpu.SemaphoreType.DMA((4,)),
            pltpu.SemaphoreType.DMA((5,)),
        ],
        compiler_params=pltpu.CompilerParams(
            collective_id=0, has_side_effects=True, vmem_limit_bytes=56 * 2**20
        ),
    )(*operands)
    return 0.5 * cot_final + out.transpose(1, 0, 2)


def solution(mesh):
    both = ("row", "col")
    in_specs = (P(None, None, both), P(None, None, both), P(both)) + (P(both, None),) * 6
    return jax.shard_map(
        functools.partial(on_device, mesh.shape["row"], mesh.shape["col"]),
        mesh=mesh,
        in_specs=in_specs,
        out_specs=P(None, None, both),
        check_vma=False,
    )
```
